256 devices in a mesh: dp: 8 (over z_hi, core), mp: 32 (over x, y, z_lo).
Axes of the slice: x: 4, y: 4, z: 8 (z_hi: 4, z_lo: 2; z = z_hi * 2 + z_lo), core: 2. Of those that a mesh axis runs over, the one named last changes fastest.
Arguments:
- tokens: bfloat16 [1024, 8192], P(('dp', 'mp')), may hold values from -6 to 6
- gate_weight: bfloat16 [8192, 26624], P('dp', 'mp'), may hold values from -0.0625 to 0.0625
- up_weight: bfloat16 [8192, 26624], P('dp', 'mp'), may hold values from -0.0625 to 0.0625
- down_weight: bfloat16 [26624, 8192], P('mp', 'dp'), may hold values from -0.0390625 to 0.0390625
- grad_mixed: bfloat16 [1024, 8192], P(('dp', 'mp')), may hold values from -6 to 6
- amax_history: float32 [26624], P('mp'), may hold values from 1 to 4
Outputs:
- grad_tokens: bfloat16 [1024, 8192], P(('dp', 'mp'))
- grad_gate: bfloat16 [8192, 26624], P('dp', 'mp')
- grad_up: bfloat16 [8192, 26624], P('dp', 'mp')
- grad_down: bfloat16 [26624, 8192], P('mp', 'dp')
- amax: float32 [26624], P('mp')
The draws below stay inside these ranges and needn't reach their ends.
All inputs are finite; a program needn't handle non-finite values.
Results may differ from the reference program's by a relative error of at most 0.0049.
Values may be sent and summed in bfloat16 or wider, within the bound.
No kernel may reach another device: no remote copies, remote signals or barrier semaphores. Data moves between devices by JAX's collectives and lax.ppermute only.
A program may use at most 128 MiB of HBM per device.

```python
import math
import jax
import jax.numpy as jnp
from jax import lax

D = 8192
FF = 26624
TOKENS = 1024


def level_of(key, shape, split, least, largest):
    loudness = 1.0
    for dim, shards_of in split:
        draws = jax.random.uniform(jax.random.fold_in(jax.random.fold_in(key, 6), dim), (shards_of,), jnp.float32, least / len(split), largest / len(split))
        loudness = loudness * jnp.repeat(jnp.exp(draws), shape[dim] // shards_of).reshape((-1,) + (1,) * (len(shape) - 1 - dim))
    return loudness


def gaussian(stream_key, extent, scale, most, shards=(), kind=jnp.bfloat16):
    entries = jax.random.normal(stream_key, extent, jnp.float32) * scale
    if len(shards) > 0:
        entries = level_of(stream_key, extent, shards, -0.22, 0.18) * entries
    return jnp.clip(entries, min=-most, max=most).astype(kind)


def setup_inputs(seed: int = 0) -> dict:
    arg_keys = jax.random.split(jax.random.key(seed), 7)
    tokens = gaussian(arg_keys[0], (TOKENS, D), 1.0, 6.0, ((0, 256),))
    gate_weight = gaussian(arg_keys[1], (D, FF), D ** -0.5, 0.0625, ((0, 8), (1, 32)))
    up_weight = gaussian(arg_keys[2], (D, FF), D ** -0.5, 0.0625, ((0, 8), (1, 32)))
    down_weight = gaussian(arg_keys[3], (FF, D), FF ** -0.5, 0.0390625, ((0, 32), (1, 8)))
    grad_mixed = gaussian(arg_keys[4], (TOKENS, D), 1.0, 6.0, ((0, 256),))
    amax_history = jnp.clip(jnp.exp(math.log(4.0) - 1.3862944 * jax.random.uniform(arg_keys[5], (FF,), jnp.float32) ** level_of(arg_keys[5], (FF,), ((0, 32),), -0.2, 0.2)), 1.0, 4.0)
    return {"tokens": tokens, "gate_weight": gate_weight, "up_weight": up_weight, "down_weight": down_weight, "grad_mixed": grad_mixed, "amax_history": amax_history}


def contract_last(left, right):
    return lax.dot_general(left, right, (((1,), (1,)), ((), ())), preferred_element_type=jnp.float32)


def contract_first(left, right):
    return lax.dot_general(left, right, (((0,), (0,)), ((), ())), preferred_element_type=jnp.float32)


def reference(tokens, gate_weight, up_weight, down_weight, grad_mixed, amax_history):
    gate = jnp.dot(tokens, gate_weight, preferred_element_type=jnp.float32)
    up = jnp.dot(tokens, up_weight, preferred_element_type=jnp.float32)
    act = jax.nn.silu(gate)
    raw = act * up
    amax = jnp.max(jnp.abs(raw), axis=0)
    bound = amax_history[None, :]
    squash = jnp.tanh(raw / bound)
    slope = 1.0 - squash * squash
    hidden = (bound * squash).astype(jnp.bfloat16)
    grad_hidden = contract_last(grad_mixed, down_weight)
    masked = grad_hidden * slope
    sig = jax.nn.sigmoid(gate)
    grad_gate_act = (masked * up * sig * (1.0 + gate * (1.0 - sig))).astype(jnp.bfloat16)
    grad_up_act = (masked * act).astype(jnp.bfloat16)
    grad_tokens = (contract_last(grad_gate_act, gate_weight) + contract_last(grad_up_act, up_weight)).astype(jnp.bfloat16)
    grad_gate = contract_first(tokens, grad_gate_act).astype(jnp.bfloat16)
    grad_up = contract_first(tokens, grad_up_act).astype(jnp.bfloat16)
    grad_down = contract_first(hidden, grad_mixed).astype(jnp.bfloat16)
    return (grad_tokens, grad_gate, grad_up, grad_down, amax)
```

```python
import jax
import jax.numpy as jnp
from jax import lax
from jax.sharding import PartitionSpec as P

NZ, NC, NX, NY, NL = 4, 2, 4, 4, 2
BF = jnp.bfloat16
F32 = jnp.float32


def index_of(z, c, x, y, l):
    return (((z * NC + c) * NX + x) * NY + y) * NL + l


def send(value, target):
    pairs = []
    for z in range(NZ):
        for c in range(NC):
            for x in range(NX):
                for y in range(NY):
                    for l in range(NL):
                        tz, tc, tx, ty, tl = target(z, c, x, y, l)
                        pairs.append(
                            (index_of(z, c, x, y, l), index_of(tz % NZ, tc % NC, tx % NX, ty % NY, tl % NL))
                        )
    return lax.ppermute(value, ("dp", "mp"), pairs)


def to_z(value, k):
    return send(value, lambda z, c, x, y, l: (z + k, c, x, y, l))


def to_y(value, k):
    return send(value, lambda z, c, x, y, l: (z, c, x, y + k, l))


def to_x_slot(value, k):
    return send(value, lambda z, c, x, y, l: (z, c, x + z + k, y, l))


def back_x_slot(value, k):
    return send(value, lambda z, c, x, y, l: (z, c, x - z - k, y, l))


def to_core(value):
    return send(value, lambda z, c, x, y, l: (z, c + 1, x, y, l))


def to_l(value):
    return send(value, lambda z, c, x, y, l: (z, c, x, y, l + 1))


def contract_last(left, right):
    return lax.dot_general(left, right, (((1,), (1,)), ((), ())), preferred_element_type=F32)


def contract_first(left, right):
    return lax.dot_general(left, right, (((0,), (0,)), ((), ())), preferred_element_type=F32)


def dot(left, right):
    return jnp.dot(left, right, preferred_element_type=F32)


def spread(shard):
    half = shard.shape[1] // 2
    a, b = shard[:, :half], shard[:, half:]
    rows = shard.shape[0]
    a_y = jnp.concatenate([a] + [to_y(a, d) for d in range(1, NY)], axis=0)
    b_x = jnp.concatenate([to_x_slot(b, k) for k in range(NX)], axis=0)
    a_all = jnp.concatenate([to_x_slot(a_y, k) for k in range(NX)], axis=0)
    b_y = [b_x] + [to_y(b_x, d) for d in range(1, NY)]
    b_all = jnp.concatenate(
        [b_y[d][k * rows : (k + 1) * rows] for k in range(NX) for d in range(NY)], axis=0
    )
    return a_all, b_all


def sum_over_z(part):
    rows = part.shape[0] // NZ
    total = part[:rows]
    for k in (2, 1, 3):
        total = total + to_z(part[k * rows : (k + 1) * rows].astype(BF), k).astype(F32)
    return total


def gather_over_z(share):
    return jnp.concatenate([share] + [to_z(share, -j) for j in range(1, NZ)], axis=0)


def total_of(pieces):
    total = pieces[0].astype(F32)
    for piece in pieces[1:]:
        total = total + piece.astype(F32)
    return total


def per_device(tokens, gate_weight, up_weight, down_weight, grad_mixed, amax_history):
    zi = lax.axis_index("dp") // NC
    ci = lax.axis_index("dp") % NC
    own_rows, width = tokens.shape
    block = width // NZ
    half = block // NC

    gate_other = to_core(gate_weight)
    up_other = to_core(up_weight)
    down_other = to_core(down_weight)

    both = jnp.concatenate([grad_mixed, tokens], axis=0)
    rolled = lax.dynamic_slice_in_dim(jnp.concatenate([both, both], axis=1), zi * block, width, 1)
    split = rolled.reshape(2 * own_rows, NZ, NC, half)
    split = jnp.where(ci == 0, split, split[:, :, ::-1])
    pieces = [split[:, k].reshape(2 * own_rows, block) for k in range(NZ)]
    got = [pieces[0]] + [to_z(pieces[k], k) for k in range(1, NZ)]
    turned = jnp.stack(got[::-1] + got[::-1])
    placed = lax.dynamic_slice_in_dim(turned, NZ - 1 - zi, NZ, 0)
    grads16 = placed[:, :own_rows].reshape(NZ * own_rows, block)
    tokens16 = placed[:, own_rows:].reshape(NZ * own_rows, block)
    here = jnp.stack([grads16, tokens16])
    there = to_l(here)
    grads32 = jnp.concatenate([here[0], there[0]], axis=0)
    tokens32 = jnp.concatenate([here[1], there[1]], axis=0)

    grads_a, grads_b = spread(grads32)
    tokens_a, tokens_b = spread(tokens32)

    grad_hidden = sum_over_z(contract_last(grads_a, down_weight) + contract_last(grads_b, down_other))
    gate = sum_over_z(dot(tokens_a, gate_weight) + dot(tokens_b, gate_other))
    up = sum_over_z(dot(tokens_a, up_weight) + dot(tokens_b, up_other))

    bound = amax_history[None, :]
    act = jax.nn.silu(gate)
    raw = act * up
    amax = jnp.max(jnp.abs(raw), axis=0)
    squash = jnp.tanh(raw / bound)
    slope = 1.0 - squash * squash
    hidden = (bound * squash).astype(BF)
    masked = grad_hidden * slope
    sig = jax.nn.sigmoid(gate)
    grad_gate_act = (masked * up * sig * (1.0 + gate * (1.0 - sig))).astype(BF)
    grad_up_act = (masked * act).astype(BF)

    gate_act = gather_over_z(grad_gate_act)
    up_act = gather_over_z(grad_up_act)
    hidden_all = gather_over_z(hidden)

    for hop in (1, 2):
        amax = jnp.maximum(amax, to_z(amax, hop))
    amax = jnp.maximum(amax, to_core(amax))

    term_a = contract_last(gate_act, gate_weight) + contract_last(up_act, up_weight)
    term_b = contract_last(gate_act, gate_other) + contract_last(up_act, up_other)
    term_a, term_b = term_a.astype(BF), term_b.astype(BF)
    rows = term_a.shape[0]
    xr, yr = rows // NX, rows // (NX * NY)
    a_x = total_of([back_x_slot(term_a[k * xr : (k + 1) * xr], k) for k in range(NX)])
    b_parts = [
        jnp.concatenate([term_b[k * xr + d * yr : k * xr + (d + 1) * yr] for k in range(NX)], axis=0)
        for d in range(NY)
    ]
    b_y = total_of([b_parts[0]] + [to_y(b_parts[d], -d) for d in range(1, NY)])
    a_y = total_of([a_x[:yr]] + [to_y(a_x[d * yr : (d + 1) * yr], -d) for d in range(1, NY)])
    b_x = total_of([back_x_slot(b_y[k * yr : (k + 1) * yr], k) for k in range(NX)])
    summed = jnp.concatenate([a_y, b_x], axis=1)
    lr = yr // NL
    mine = (summed[:lr] + to_l(summed[lr:])).astype(BF)

    mine = mine.reshape(NZ, own_rows, block)
    turned = lax.dynamic_slice_in_dim(jnp.concatenate([mine, mine], axis=0), zi, NZ, 0)
    got = [turned[0]] + [to_z(turned[k], k) for k in range(1, NZ)]
    doubled = jnp.stack(got[::-1] + got[::-1])
    placed = lax.dynamic_slice_in_dim(doubled, NZ - 1 - zi, NZ, 0)
    placed = placed.reshape(NZ, own_rows, NC, half)
    placed = jnp.where(ci == 0, placed, placed[:, :, ::-1])
    grad_tokens = placed.transpose(1, 0, 2, 3).reshape(own_rows, width)

    token_cols = jnp.concatenate([tokens_a, to_core(tokens_b)], axis=0)
    grad_cols = jnp.concatenate([grads_a, to_core(grads_b)], axis=0)
    gate_act2 = jnp.concatenate([gate_act, to_core(gate_act)], axis=0)
    up_act2 = jnp.concatenate([up_act, to_core(up_act)], axis=0)
    hidden2 = jnp.concatenate([hidden_all, to_core(hidden_all)], axis=0)
    grad_gate = contract_first(token_cols, gate_act2).astype(BF)
    grad_up = contract_first(token_cols, up_act2).astype(BF)
    grad_down = contract_first(hidden2, grad_cols).astype(BF)
    return (grad_tokens, grad_gate, grad_up, grad_down, amax)


def solution(mesh):
    return jax.shard_map(
        per_device,
        mesh=mesh,
        in_specs=(
            P(("dp", "mp"), None),
            P("dp", "mp"),
            P("dp", "mp"),
            P("mp", "dp"),
            P(("dp", "mp"), None),
            P("mp"),
        ),
        out_specs=(P(("dp", "mp"), None), P("dp", "mp"), P("dp", "mp"), P("mp", "dp"), P("mp")),
        check_vma=False,
    )
```

```python
import jax
import jax.numpy as jnp
from jax import lax
from jax.sharding import Mesh, PartitionSpec as P

NZ, NC, NX, NY, NL = 4, 2, 4, 4, 2
AXES = ("z", "c", "x", "y", "l")
MP = ("x", "y", "l")
BF = jnp.bfloat16
F32 = jnp.float32


def shift(value, axis, k):
    n = {"z": NZ, "c": NC, "l": NL}[axis]
    return lax.ppermute(value, axis, [(i, (i + k) % n) for i in range(n)])


def swap(value):
    return shift(value, "c", 1)


def contract_last(left, right):
    return lax.dot_general(left, right, (((1,), (1,)), ((), ())), preferred_element_type=F32)


def contract_first(left, right):
    return lax.dot_general(left, right, (((0,), (0,)), ((), ())), preferred_element_type=F32)


def dot(left, right):
    return jnp.dot(left, right, preferred_element_type=F32)


def exchange(value, axis):
    return lax.all_to_all(value, axis, split_axis=0, concat_axis=0, tiled=True)


def sum_over_z(part):
    rows = part.shape[0] // NZ
    total = part[:rows]
    for k in (2, 1, 3):
        total = total + shift(part[k * rows : (k + 1) * rows].astype(BF), "z", k).astype(F32)
    return total


def gather_over_z(share):
    return jnp.concatenate([share] + [shift(share, "z", -j) for j in range(1, NZ)], axis=0)


def per_device(tokens, gate_weight, up_weight, down_weight, grad_mixed, amax_history):
    zi = lax.axis_index("z")
    ci = lax.axis_index("c")
    own_rows, width = tokens.shape
    block = width // NZ
    half = block // NC
    few = NZ * own_rows
    peers = NX * NY * NL
    group = peers * few // NZ

    gate_other = swap(gate_weight)
    up_other = swap(up_weight)
    down_other = swap(down_weight)

    both = jnp.concatenate([grad_mixed, tokens], axis=0).reshape(2 * own_rows, NZ, block)
    placed = exchange(both.transpose(1, 0, 2), "z")
    grads16 = placed[:, :own_rows].reshape(few, block)
    tokens16 = placed[:, own_rows:].reshape(few, block)

    def spread(shard):
        whole = exchange(jnp.broadcast_to(shard[None], (peers, few, block)), MP)
        groups = whole.reshape(NZ, group, block)
        halves = []
        for c in (ci, 1 - ci):
            halves.append(
                jnp.concatenate(
                    [
                        lax.dynamic_slice(groups, ((zi + j) % NZ, 0, c * half), (1, group, half))[0]
                        for j in range(NZ)
                    ],
                    axis=0,
                )
            )
        return halves

    grads_a, grads_b = spread(grads16)
    tokens_a, tokens_b = spread(tokens16)

    grad_hidden = sum_over_z(contract_last(grads_a, down_weight) + contract_last(grads_b, down_other))
    gate = sum_over_z(dot(tokens_a, gate_weight) + dot(tokens_b, gate_other))
    up = sum_over_z(dot(tokens_a, up_weight) + dot(tokens_b, up_other))

    bound = amax_history[None, :]
    act = jax.nn.silu(gate)
    raw = act * up
    amax = jnp.max(jnp.abs(raw), axis=0)
    squash = jnp.tanh(raw / bound)
    slope = 1.0 - squash * squash
    hidden = (bound * squash).astype(BF)
    masked = grad_hidden * slope
    sig = jax.nn.sigmoid(gate)
    grad_gate_act = (masked * up * sig * (1.0 + gate * (1.0 - sig))).astype(BF)
    grad_up_act = (masked * act).astype(BF)

    gate_act = gather_over_z(grad_gate_act)
    up_act = gather_over_z(grad_up_act)
    hidden_all = gather_over_z(hidden)

    for hop in (1, 2):
        amax = jnp.maximum(amax, shift(amax, "z", hop))
    amax = jnp.maximum(amax, swap(amax))

    term_a = contract_last(gate_act, gate_weight) + contract_last(up_act, up_weight)
    term_b = contract_last(gate_act, gate_other) + contract_last(up_act, up_other)
    terms = jnp.stack([term_a.astype(BF), term_b.astype(BF)]).reshape(2, NZ, group, half)
    halves = [
        jnp.concatenate(
            [
                lax.dynamic_slice(terms, (c, (j - zi) % NZ, 0, 0), (1, 1, group, half))[0, 0]
                for j in range(NZ)
            ],
            axis=0,
        )
        for c in (ci, 1 - ci)
    ]
    sent = jnp.concatenate(halves, axis=1).reshape(peers, few, block)
    mine = jnp.sum(exchange(sent, MP).astype(F32), axis=0).astype(BF)

    back = exchange(mine.reshape(NZ, own_rows, block), "z")
    grad_tokens = back.transpose(1, 0, 2).reshape(own_rows, width)

    token_cols = jnp.concatenate([tokens_a, swap(tokens_b)], axis=0)
    grad_cols = jnp.concatenate([grads_a, swap(grads_b)], axis=0)
    gate_act2 = jnp.concatenate([gate_act, swap(gate_act)], axis=0)
    up_act2 = jnp.concatenate([up_act, swap(up_act)], axis=0)
    hidden2 = jnp.concatenate([hidden_all, swap(hidden_all)], axis=0)
    grad_gate = contract_first(token_cols, gate_act2).astype(BF)
    grad_up = contract_first(token_cols, up_act2).astype(BF)
    grad_down = contract_first(hidden2, grad_cols).astype(BF)
    return (grad_tokens, grad_gate, grad_up, grad_down, amax)


def solution(mesh):
    split = Mesh(mesh.devices.reshape(NZ, NC, NX, NY, NL), AXES)
    rows, units = ("z", "c"), MP
    return jax.shard_map(
        per_device,
        mesh=split,
        in_specs=(
            P(AXES, None),
            P(rows, units),
            P(rows, units),
            P(units, rows),
            P(AXES, None),
            P(units),
        ),
        out_specs=(P(AXES, None), P(rows, units), P(rows, units), P(units, rows), P(units)),
        check_vma=False,
    )
```

```python
import jax
import jax.numpy as jnp
from jax import lax
from jax.sharding import Mesh, PartitionSpec as P

NZ, NC, NX, NY, NL = 4, 2, 4, 4, 2
AXES = ("z", "c", "x", "y", "l")
MP = ("x", "y", "l")
BF = jnp.bfloat16
F32 = jnp.float32


def shift(value, axis, k):
    n = {"z": NZ, "c": NC, "l": NL}[axis]
    return lax.ppermute(value, axis, [(i, (i + k) % n) for i in range(n)])


def swap(value):
    return shift(value, "c", 1)


def contract_last(left, right):
    return lax.dot_general(left, right, (((1,), (1,)), ((), ())), preferred_element_type=F32)


def contract_first(left, right):
    return lax.dot_general(left, right, (((0,), (0,)), ((), ())), preferred_element_type=F32)


def dot(left, right):
    return jnp.dot(left, right, preferred_element_type=F32)


def exchange(value, axis):
    return lax.all_to_all(value, axis, split_axis=0, concat_axis=0, tiled=True)


def after(value, *others):
    for other in others:
        corner = lax.slice(other, (0,) * other.ndim, (1,) * other.ndim).reshape(())
        value = value + (0 * corner).astype(value.dtype)
    return value


def sum_over_z(parts, zi):
    rows = parts[0].shape[0] // NZ

    def group(k):
        return jnp.stack([lax.dynamic_slice_in_dim(p, ((zi + k) % NZ) * rows, rows, 0) for p in parts])

    total = group(0)
    for k in (2, 1, 3):
        total = total + shift(group(k).astype(BF), "z", k).astype(F32)
    return [total[i] for i in range(len(parts))]


def gather_over_z(shares, zi):
    whole = jnp.stack(shares)
    got = [whole] + [shift(whole, "z", -j) for j in (2, 1, 3)]
    pieces = [got[0], got[2], got[1], got[3]]
    rows = shares[0].shape[0]
    outs = []
    for i in range(len(shares)):
        twice = jnp.concatenate([p[i] for p in pieces + pieces], axis=0)
        outs.append(lax.dynamic_slice_in_dim(twice, ((NZ - zi) % NZ) * rows, NZ * rows, 0))
    return outs


def per_device(tokens, gate_weight, up_weight, down_weight, grad_mixed, amax_history):
    zi = lax.axis_index("z")
    ci = lax.axis_index("c")
    own_rows, width = tokens.shape
    block = width // NZ
    half = block // NC
    few = NZ * NL * own_rows
    peers = NX * NY

    gate_other = swap(gate_weight)
    up_other = swap(up_weight)
    down_other = swap(down_weight)

    def own_first(value):
        return jnp.where(ci == 0, value, jnp.concatenate([value[..., half:], value[..., :half]], axis=-1))

    both = jnp.concatenate([grad_mixed, tokens], axis=0).reshape(2 * own_rows, NZ, 1, block)
    both = jnp.broadcast_to(both.transpose(1, 2, 0, 3), (NZ, NL, 2 * own_rows, block))
    placed = own_first(exchange(both.reshape(NZ * NL, 2 * own_rows, block), ("z", "l")))
    grads_few = placed[:, :own_rows].reshape(few, block)
    tokens_few = placed[:, own_rows:].reshape(few, block)

    def spread(shard):
        whole = exchange(jnp.broadcast_to(shard[None], (peers, few, block)), ("x", "y"))
        whole = whole.reshape(peers * few, block)
        return whole[:, :half], whole[:, half:]

    tokens_a, tokens_b = spread(tokens_few)
    gate_part = dot(tokens_a, gate_weight) + dot(tokens_b, gate_other)
    up_part = dot(tokens_a, up_weight) + dot(tokens_b, up_other)
    gate, up = sum_over_z([gate_part, up_part], zi)
    grads_a, grads_b = spread(after(grads_few, tokens_a))
    hidden_part = contract_last(grads_a, down_weight) + contract_last(grads_b, down_other)
    (grad_hidden,) = sum_over_z([after(hidden_part, gate)], zi)

    bound = amax_history[None, :]
    act = jax.nn.silu(gate)
    raw = act * up
    amax = jnp.max(jnp.abs(raw), axis=0)
    squash = jnp.tanh(raw / bound)
    slope = 1.0 - squash * squash
    hidden = (bound * squash).astype(BF)
    masked = grad_hidden * slope
    sig = jax.nn.sigmoid(gate)
    grad_gate_act = (masked * up * sig * (1.0 + gate * (1.0 - sig))).astype(BF)
    grad_up_act = (masked * act).astype(BF)

    gate_act, up_act = gather_over_z([grad_gate_act, grad_up_act], zi)
    (hidden_all,) = gather_over_z([after(hidden, gate_act)], zi)

    amax = jnp.maximum(
        jnp.maximum(amax, shift(amax, "z", 1)), jnp.maximum(shift(amax, "z", 2), shift(amax, "z", 3))
    )
    amax = jnp.maximum(amax, swap(amax))

    term_a = contract_last(gate_act, gate_weight) + contract_last(up_act, up_weight)
    term_b = contract_last(gate_act, gate_other) + contract_last(up_act, up_other)
    sent = jnp.concatenate([term_a.astype(BF), term_b.astype(BF)], axis=1).reshape(peers, few, block)
    mine = jnp.sum(exchange(sent, ("x", "y")).astype(F32), axis=0)

    token_cols = jnp.concatenate([tokens_a, swap(tokens_b)], axis=0)
    grad_cols = jnp.concatenate([grads_a, swap(grads_b)], axis=0)
    gate_act2 = jnp.concatenate([gate_act, swap(gate_act)], axis=0)
    up_act2 = jnp.concatenate([up_act, swap(up_act)], axis=0)
    hidden2 = jnp.concatenate([hidden_all, swap(hidden_all)], axis=0)
    grad_gate = contract_first(token_cols, gate_act2).astype(BF)
    grad_up = contract_first(token_cols, up_act2).astype(BF)
    grad_down = contract_first(hidden2, grad_cols).astype(BF)

    mine = after(mine, grad_gate, grad_up)
    back = exchange(mine.reshape(NZ * NL, own_rows, block), ("z", "l"))
    back = own_first(jnp.sum(back.reshape(NZ, NL, own_rows, block), axis=1).astype(BF))
    grad_tokens = back.transpose(1, 0, 2).reshape(own_rows, width)
    return (grad_tokens, grad_gate, grad_up, grad_down, amax)


def solution(mesh):
    split = Mesh(mesh.devices.reshape(NZ, NC, NX, NY, NL), AXES)
    rows, units = ("z", "c"), MP
    return jax.shard_map(
        per_device,
        mesh=split,
        in_specs=(
            P(AXES, None),
            P(rows, units),
            P(rows, units),
            P(units, rows),
            P(AXES, None),
            P(units),
        ),
        out_specs=(P(AXES, None), P(rows, units), P(rows, units), P(units, rows), P(units)),
        check_vma=False,
    )
```

```python
import jax
import jax.numpy as jnp
from jax import lax
from jax.experimental import pallas as pl
from jax.experimental.pallas import tpu as pltpu
from jax.sharding import Mesh, PartitionSpec as P

NZ, NC, NX, NY, NL = 4, 2, 4, 4, 2
AXES = ("z", "c", "x", "y", "l")
MP = ("x", "y", "l")
BF = jnp.bfloat16
F32 = jnp.float32


def shift(value, axis, k):
    n = {"z": NZ, "c": NC, "l": NL}[axis]
    return lax.ppermute(value, axis, [(i, (i + k) % n) for i in range(n)])


def swap(value):
    return shift(value, "c", 1)


def dot(left, right):
    return jnp.dot(left, right, preferred_element_type=F32)


def exchange(value, axis):
    return lax.all_to_all(value, axis, split_axis=0, concat_axis=0, tiled=True)


VMEM_BYTES = 48 * 2**20


def params():
    return pltpu.CompilerParams(vmem_limit_bytes=VMEM_BYTES)


def dot_nt(left, right):
    return lax.dot_general(left, right, (((1,), (1,)), ((), ())), preferred_element_type=F32)


def project(zi, columns, own, other):
    n = len(own)
    rows, width = columns.shape
    units = own[0].shape[0]
    steps, group = 4, rows // NZ
    tile = width // steps

    def kernel(z_ref, c_ref, *refs):
        own_refs, other_refs = refs[:n], refs[n : 2 * n]
        out, sends = refs[2 * n], refs[2 * n + 1 : 2 * n + NZ]
        totals = refs[2 * n + NZ :]
        step = pl.program_id(0)

        @pl.when(step == 0)
        def _():
            for total, w in zip(totals, own_refs):
                total[...] = dot_nt(c_ref[...], w[...])

        @pl.when((step > 0) & (step < steps // 2))
        def _():
            for total, w in zip(totals, own_refs):
                total[...] += dot_nt(c_ref[...], w[...])

        @pl.when(step >= steps // 2)
        def _():
            for total, w in zip(totals, other_refs):
                total[...] += dot_nt(c_ref[...], w[...])

        @pl.when(step == steps - 1)
        def _():
            for k in range(NZ):
                start = pl.multiple_of(lax.rem(z_ref[0] + k, NZ) * group, group)
                parts = [total[pl.ds(start, group), :] for total in totals]
                value = jnp.concatenate(parts, axis=1) if n > 1 else parts[0]
                if k == 0:
                    out[...] = value
                else:
                    sends[k - 1][...] = value.astype(BF)

    half = steps // 2
    whole = pl.BlockSpec((group, n * units), lambda i, z: (0, 0))
    return pl.pallas_call(
        kernel,
        grid_spec=pltpu.PrefetchScalarGridSpec(
            num_scalar_prefetch=1,
            grid=(steps,),
            in_specs=[pl.BlockSpec((rows, tile), lambda i, z: (0, i))]
            + [pl.BlockSpec((units, tile), lambda i, z: (0, jnp.minimum(i, half - 1)))] * n
            + [pl.BlockSpec((units, tile), lambda i, z: (0, jnp.maximum(i - half, 0)))] * n,
            out_specs=[whole] * NZ,
            scratch_shapes=[pltpu.VMEM((rows, units), F32)] * n,
        ),
        out_shape=[jax.ShapeDtypeStruct((group, n * units), F32)]
        + [jax.ShapeDtypeStruct((group, n * units), BF)] * (NZ - 1),
        compiler_params=params(),
        cost_estimate=pl.CostEstimate(
            flops=2 * rows * width * units * n,
            bytes_accessed=2 * (rows * width + width * units * n) + 10 * group * n * units,
            transcendentals=0,
        ),
    )(zi, columns, *own, *other)


def activations(both, hidden_grad, bound):
    rows, units = hidden_grad[0].shape
    steps = 2
    tile = rows // steps

    def kernel(*refs):
        b_refs, h_refs, bound_ref = refs[:NZ], refs[NZ : 2 * NZ], refs[2 * NZ]
        acts_ref, hidden_ref, amax_ref = refs[2 * NZ + 1 :]
        total = b_refs[0][...]
        for ref in b_refs[1:]:
            total = total + ref[...].astype(F32)
        grad = h_refs[0][...]
        for ref in h_refs[1:]:
            grad = grad + ref[...].astype(F32)
        gate, up = total[:, :units], total[:, units:]
        limit = bound_ref[...]
        sig = jax.nn.sigmoid(gate)
        act = gate * sig
        raw = act * up
        top = jnp.max(jnp.abs(raw), axis=0, keepdims=True)
        step = pl.program_id(0)

        @pl.when(step == 0)
        def _():
            amax_ref[...] = top

        @pl.when(step > 0)
        def _():
            amax_ref[...] = jnp.maximum(amax_ref[...], top)

        squash = jnp.tanh(raw / limit)
        masked = grad * (1.0 - squash * squash)
        hidden_ref[...] = (limit * squash).astype(BF)
        gate_act = masked * up * sig * (1.0 + gate * (1.0 - sig))
        acts_ref[...] = jnp.concatenate([gate_act, masked * act], axis=1).astype(BF)

    wide = pl.BlockSpec((tile, 2 * units), lambda i: (i, 0))
    narrow = pl.BlockSpec((tile, units), lambda i: (i, 0))
    line = pl.BlockSpec((1, units), lambda i: (0, 0))
    return pl.pallas_call(
        kernel,
        grid=(steps,),
        in_specs=[wide] * NZ + [narrow] * NZ + [line],
        out_specs=[wide, narrow, line],
        out_shape=[
            jax.ShapeDtypeStruct((rows, 2 * units), BF),
            jax.ShapeDtypeStruct((rows, units), BF),
            jax.ShapeDtypeStruct((1, units), F32),
        ],
        compiler_params=params(),
        cost_estimate=pl.CostEstimate(
            flops=40 * rows * units, bytes_accessed=34 * rows * units, transcendentals=2 * rows * units
        ),
    )(*both, *hidden_grad, bound)


def input_terms(zi, pieces, own, other, ties=()):
    group, both = pieces[0].shape
    units, depth = own[0].shape
    steps = 4
    tile = 2 * depth // steps
    half = steps // 2
    rows = NZ * group

    def kernel(z_ref, *refs):
        p_refs, w_refs = refs[:NZ], refs[NZ : NZ + 4]
        out_ref, all_ref, stacked = refs[NZ + 4 + len(ties) :]
        step = pl.program_id(0)

        @pl.when(step == 0)
        def _():
            for j in range(NZ):
                start = pl.multiple_of(lax.rem(z_ref[0] + j, NZ) * group, group)
                all_ref[pl.ds(start, group), :] = p_refs[j][...]

        @pl.when(step < half)
        def _():
            stacked[:units, :] = w_refs[0][...]
            stacked[units:, :] = w_refs[1][...]

        @pl.when(step >= half)
        def _():
            stacked[:units, :] = w_refs[2][...]
            stacked[units:, :] = w_refs[3][...]

        out_ref[...] = dot(all_ref[...], stacked[...]).astype(BF)

    return pl.pallas_call(
        kernel,
        grid_spec=pltpu.PrefetchScalarGridSpec(
            num_scalar_prefetch=1,
            grid=(steps,),
            in_specs=[pl.BlockSpec((group, both), lambda i, z: (0, 0))] * NZ
            + [pl.BlockSpec((units, tile), lambda i, z: (0, jnp.minimum(i, half - 1)))] * 2
            + [pl.BlockSpec((units, tile), lambda i, z: (0, jnp.maximum(i - half, 0)))] * 2
            + [pl.BlockSpec(memory_space=pl.ANY)] * len(ties),
            out_specs=[
                pl.BlockSpec((rows, tile), lambda i, z: (0, i)),
                pl.BlockSpec((rows, both), lambda i, z: (0, 0)),
            ],
            scratch_shapes=[pltpu.VMEM((both, tile), BF)],
        ),
        out_shape=[
            jax.ShapeDtypeStruct((rows, 2 * depth), BF),
            jax.ShapeDtypeStruct((rows, both), BF),
        ],
        compiler_params=params(),
        cost_estimate=pl.CostEstimate(
            flops=4 * rows * both * depth,
            bytes_accessed=4 * rows * both + 4 * rows * depth + 4 * both * depth,
            transcendentals=0,
        ),
    )(zi, *pieces, *own, *other, *ties)


def repeated(shard, peers, ties=()):
    rows, width = shard.shape
    steps = 4

    def kernel(s_ref, *refs):
        refs[-1][...] = jnp.broadcast_to(s_ref[...][None], refs[-1].shape)

    return pl.pallas_call(
        kernel,
        grid=(steps,),
        in_specs=[pl.BlockSpec((rows, width), lambda i: (0, 0))]
        + [pl.BlockSpec(memory_space=pl.ANY)] * len(ties),
        out_specs=pl.BlockSpec((peers // steps, rows, width), lambda i: (i, 0, 0)),
        out_shape=jax.ShapeDtypeStruct((peers, rows, width), shard.dtype),
        cost_estimate=pl.CostEstimate(flops=0, bytes_accessed=2 * peers * rows * width, transcendentals=0),
    )(shard, *ties)


def summed(pieces, ties=()):
    peers, rows, width = pieces.shape
    steps = 4
    tile = width // steps

    def kernel(p_ref, *refs):
        refs[-1][...] = jnp.sum(p_ref[...].astype(F32), axis=0)

    return pl.pallas_call(
        kernel,
        grid=(steps,),
        in_specs=[pl.BlockSpec((peers, rows, tile), lambda i: (0, 0, i))]
        + [pl.BlockSpec(memory_space=pl.ANY)] * len(ties),
        out_specs=pl.BlockSpec((rows, tile), lambda i: (0, i)),
        out_shape=jax.ShapeDtypeStruct((rows, width), F32),
        cost_estimate=pl.CostEstimate(
            flops=peers * rows * width, bytes_accessed=2 * peers * rows * width, transcendentals=0
        ),
    )(pieces, *ties)


def stacked_rows(first, second, ties=()):
    rows, width = first.shape

    def kernel(a_ref, b_ref, *refs):
        refs[-1][:rows, :] = a_ref[...]
        refs[-1][rows:, :] = b_ref[...]

    whole = pl.BlockSpec((rows, width), lambda: (0, 0))
    return pl.pallas_call(
        kernel,
        in_specs=[whole, whole] + [pl.BlockSpec(memory_space=pl.ANY)] * len(ties),
        out_specs=pl.BlockSpec((2 * rows, width), lambda: (0, 0)),
        out_shape=jax.ShapeDtypeStruct((2 * rows, width), first.dtype),
        cost_estimate=pl.CostEstimate(flops=0, bytes_accessed=8 * rows * width, transcendentals=0),
    )(first, second, *ties)


def by_chunk_and_z(zi, pieces):
    both, units = pieces[0].shape
    rows = both // 2

    def kernel(z_ref, *refs):
        for j in range(NZ):
            owner = lax.rem(z_ref[0] + j, NZ)
            for chunk in range(2):
                start = pl.multiple_of(chunk * NZ * rows + owner * rows, rows)
                refs[NZ][pl.ds(start, rows), :] = refs[j][chunk * rows : (chunk + 1) * rows, :]

    whole = pl.BlockSpec((both, units), lambda i, z: (0, 0))
    return pl.pallas_call(
        kernel,
        grid_spec=pltpu.PrefetchScalarGridSpec(
            num_scalar_prefetch=1,
            grid=(1,),
            in_specs=[whole] * NZ,
            out_specs=pl.BlockSpec((NZ * both, units), lambda i, z: (0, 0)),
        ),
        out_shape=jax.ShapeDtypeStruct((NZ * both, units), BF),
        cost_estimate=pl.CostEstimate(flops=0, bytes_accessed=16 * both * units, transcendentals=0),
    )(zi, *pieces)


def weight_gradients(terms, outs, depth):
    rows = terms[0][2].shape[0]
    wide = terms[0][0].shape[1]
    units = wide // outs
    steps = 4
    tile = depth // steps
    n = len(terms)

    def kernel(*refs):
        lefts, rights, results, turned = refs[:n], refs[n : 2 * n], refs[2 * n : 2 * n + outs], refs[-1]

        @pl.when(pl.program_id(0) == 0)
        def _():
            for i in range(n):
                turned[:, i * rows : (i + 1) * rows] = lefts[i][...].T

        right = jnp.concatenate([r[...] for r in rights], axis=0)
        for o in range(outs):
            results[o][...] = dot(turned[o * units : (o + 1) * units, :], right).astype(BF)

    def left_spec(block):
        return pl.BlockSpec((rows, wide), lambda i: (block, 0))

    def right_spec(half):
        return pl.BlockSpec((rows, tile), lambda i: (0, half * steps + i))

    return pl.pallas_call(
        kernel,
        grid=(steps,),
        in_specs=[left_spec(t[1]) for t in terms] + [right_spec(t[3]) for t in terms],
        out_specs=[pl.BlockSpec((units, tile), lambda i: (0, i))] * outs,
        out_shape=[jax.ShapeDtypeStruct((units, depth), BF)] * outs,
        scratch_shapes=[pltpu.VMEM((wide, n * rows), BF)],
        compiler_params=params(),
        cost_estimate=pl.CostEstimate(
            flops=2 * n * rows * wide * depth,
            bytes_accessed=2 * (n * rows * (wide + depth) + wide * depth),
            transcendentals=0,
        ),
    )(*[t[0] for t in terms], *[t[2] for t in terms])


def sum_parts(pieces):
    got = {k: shift(pieces[k], "z", k) for k in (2, 1, 3)}
    return [pieces[0]] + [got[k] for k in (1, 2, 3)]


def gather_parts(share):
    got = {j: shift(share, "z", -j) for j in (2, 1, 3)}
    return [share] + [got[j] for j in (1, 2, 3)]


def per_device(tokens, gate_weight, up_weight, down_weight, grad_mixed, amax_history):
    zi = lax.axis_index("z")
    ci = lax.axis_index("c")
    zs = zi.astype(jnp.int32).reshape((1,))
    own_rows, width = tokens.shape
    block = width // NZ
    half = block // NC
    few = NZ * NL * own_rows
    peers = NX * NY
    chunk = few // 2

    gate_t, up_t = gate_weight.T, up_weight.T
    gate_other = swap(gate_t)
    up_other = swap(up_t)
    down_other = swap(down_weight)

    def own_first(value):
        return jnp.where(ci == 0, value, jnp.concatenate([value[..., half:], value[..., :half]], axis=-1))

    both = jnp.concatenate([grad_mixed, tokens], axis=0).reshape(2 * own_rows, NZ, 1, block)
    both = jnp.broadcast_to(both.transpose(1, 2, 0, 3), (NZ, NL, 2 * own_rows, block))
    placed = own_first(exchange(both.reshape(NZ * NL, 2 * own_rows, block), ("z", "l")))
    grads_few = placed[:, :own_rows].reshape(few, block)
    tokens_few = placed[:, own_rows:].reshape(few, block)

    def spread(shard, ties):
        whole = exchange(repeated(shard, peers, ties), ("x", "y"))
        return whole.reshape(peers * chunk, block)

    tokens_a = spread(tokens_few[:chunk], ())
    grads_a = spread(grads_few[:chunk], (tokens_a,))
    tokens_b = spread(tokens_few[chunk:], (grads_a,))
    grads_b = spread(grads_few[chunk:], (tokens_b,))

    own, other = [gate_t, up_t], [gate_other, up_other]
    bound = amax_history[None, :]

    def middle(tokens_all, grads_all):
        both_parts = sum_parts(project(zs, tokens_all, own, other))
        hidden_parts = sum_parts(project(zs, grads_all, [down_weight], [down_other]))
        return activations(both_parts, hidden_parts, bound)

    acts_a, hidden_a, amax_a = middle(tokens_a, grads_a)
    terms_a, acts_all_a = input_terms(zs, gather_parts(acts_a), own, other, (grads_b,))
    acts_b, hidden_b, amax_b = middle(tokens_b, grads_b)
    terms_b, acts_all_b = input_terms(zs, gather_parts(acts_b), own, other)

    sums_a = exchange(terms_a.reshape(peers, chunk, block), ("x", "y"))
    sums_b = exchange(terms_b.reshape(peers, chunk, block), ("x", "y"))

    hidden_pieces = gather_parts(stacked_rows(hidden_a, hidden_b, (terms_b,)))
    hidden_all = by_chunk_and_z(zs, hidden_pieces)

    amax = jnp.maximum(amax_a, amax_b)[0]
    amax = jnp.maximum(
        jnp.maximum(amax, shift(amax, "z", 1)), jnp.maximum(shift(amax, "z", 2), shift(amax, "z", 3))
    )
    amax = jnp.maximum(amax, swap(amax))

    grad_gate, grad_up = weight_gradients(
        [
            (acts_all_a, 0, tokens_a, 0),
            (acts_all_b, 0, tokens_b, 0),
            (swap(acts_all_a), 0, swap(tokens_a), 1),
            (swap(acts_all_b), 0, swap(tokens_b), 1),
        ],
        2,
        half,
    )
    hidden_other = swap(hidden_all)
    grads_other = [swap(grads_a), swap(grads_b)]
    (grad_down,) = weight_gradients(
        [
            (hidden_all, 0, grads_a, 0),
            (hidden_all, 1, grads_b, 0),
            (hidden_other, 0, grads_other[0], 1),
            (hidden_other, 1, grads_other[1], 1),
        ],
        1,
        half,
    )

    mine = [summed(sums_a), summed(sums_b, (grad_gate,))]
    back = exchange(jnp.concatenate(mine, axis=0).reshape(NZ * NL, own_rows, block), ("z", "l"))
    back = own_first(jnp.sum(back.reshape(NZ, NL, own_rows, block), axis=1).astype(BF))
    grad_tokens = back.transpose(1, 0, 2).reshape(own_rows, width)
    return (grad_tokens, grad_gate.T, grad_up.T, grad_down, amax)


def solution(mesh):
    split = Mesh(mesh.devices.reshape(NZ, NC, NX, NY, NL), AXES)
    rows, units = ("z", "c"), MP
    return jax.shard_map(
        per_device,
        mesh=split,
        in_specs=(
            P(AXES, None),
            P(rows, units),
            P(rows, units),
            P(units, rows),
            P(AXES, None),
            P(units),
        ),
        out_specs=(P(AXES, None), P(rows, units), P(rows, units), P(units, rows), P(units)),
        check_vma=False,
    )
```

```python
import jax
import jax.numpy as jnp
from jax import lax
from jax.experimental import pallas as pl
from jax.experimental.pallas import tpu as pltpu
from jax.sharding import Mesh, PartitionSpec as P

NZ, NC, NX, NY, NL = 4, 2, 4, 4, 2
AXES = ("z", "c", "x", "y", "l")
MP = ("x", "y", "l")
BF = jnp.bfloat16
F32 = jnp.float32


def shift(value, axis, k):
    n = {"z": NZ, "c": NC, "l": NL}[axis]
    return lax.ppermute(value, axis, [(i, (i + k) % n) for i in range(n)])


def swap(value):
    return shift(value, "c", 1)


def dot(left, right):
    return jnp.dot(left, right, preferred_element_type=F32)


def exchange(value, axis):
    return lax.all_to_all(value, axis, split_axis=0, concat_axis=0, tiled=True)


VMEM_BYTES = 48 * 2**20


def params():
    return pltpu.CompilerParams(vmem_limit_bytes=VMEM_BYTES)


def dot_nt(left, right):
    return lax.dot_general(left, right, (((1,), (1,)), ((), ())), preferred_element_type=F32)


def project(zi, pairs, own, other, ties=()):
    n = len(own)
    peers, few, width = pairs.shape
    rows = peers * few // 2
    units = own[0].shape[0]
    steps, group = 4, rows // NZ
    tile = width // steps

    def kernel(z_ref, t_ref, g_ref, *refs):
        own_refs, other_refs = refs[:n], refs[n : 2 * n]
        refs = refs[2 * n + len(ties) :]
        out, sends, totals = refs[0], refs[1:NZ], refs[NZ:]
        step = pl.program_id(0)
        columns = [t_ref[...].reshape(rows, tile)] * 2 + [g_ref[...].reshape(rows, tile)]

        @pl.when(step == 0)
        def _():
            for total, c, w in zip(totals, columns, own_refs):
                total[...] = dot_nt(c, w[...])

        @pl.when((step > 0) & (step < steps // 2))
        def _():
            for total, c, w in zip(totals, columns, own_refs):
                total[...] += dot_nt(c, w[...])

        @pl.when(step >= steps // 2)
        def _():
            for total, c, w in zip(totals, columns, other_refs):
                total[...] += dot_nt(c, w[...])

        @pl.when(step == steps - 1)
        def _():
            for k in range(NZ):
                start = pl.multiple_of(lax.rem(z_ref[0] + k, NZ) * group, group)
                value = jnp.concatenate([total[pl.ds(start, group), :] for total in totals], axis=1)
                if k == 0:
                    out[...] = value
                else:
                    sends[k - 1][...] = value.astype(BF)

    half = steps // 2
    whole = pl.BlockSpec((group, n * units), lambda i, z: (0, 0))
    return pl.pallas_call(
        kernel,
        grid_spec=pltpu.PrefetchScalarGridSpec(
            num_scalar_prefetch=1,
            grid=(steps,),
            in_specs=[
                pl.BlockSpec((peers, few // 2, tile), lambda i, z: (0, 0, i)),
                pl.BlockSpec((peers, few // 2, tile), lambda i, z: (0, 1, i)),
            ]
            + [pl.BlockSpec((units, tile), lambda i, z: (0, jnp.minimum(i, half - 1)))] * n
            + [pl.BlockSpec((units, tile), lambda i, z: (0, jnp.maximum(i - half, 0)))] * n
            + [pl.BlockSpec(memory_space=pl.ANY)] * len(ties),
            out_specs=[whole] * NZ,
            scratch_shapes=[pltpu.VMEM((rows, units), F32)] * n,
        ),
        out_shape=[jax.ShapeDtypeStruct((group, n * units), F32)]
        + [jax.ShapeDtypeStruct((group, n * units), BF)] * (NZ - 1),
        compiler_params=params(),
        cost_estimate=pl.CostEstimate(
            flops=2 * rows * width * units * n,
            bytes_accessed=2 * (2 * rows * width + width * units * n) + 10 * group * n * units,
            transcendentals=0,
        ),
    )(zi, pairs, pairs, *own, *other, *ties)


def activations(parts, bound):
    rows, units = parts[0].shape[0], bound.shape[1]
    steps = 2
    tile = rows // steps

    def kernel(*refs):
        bound_ref, acts_ref, hidden_ref, amax_ref = refs[NZ:]
        total = refs[0][...]
        for ref in refs[1:NZ]:
            total = total + ref[...].astype(F32)
        gate, up, grad = (total[:, i * units : (i + 1) * units] for i in range(3))
        limit = bound_ref[...]
        sig = jax.nn.sigmoid(gate)
        act = gate * sig
        raw = act * up
        top = jnp.max(jnp.abs(raw), axis=0, keepdims=True)
        step = pl.program_id(0)

        @pl.when(step == 0)
        def _():
            amax_ref[...] = top

        @pl.when(step > 0)
        def _():
            amax_ref[...] = jnp.maximum(amax_ref[...], top)

        squash = jnp.tanh(raw / limit)
        masked = grad * (1.0 - squash * squash)
        hidden_ref[...] = (limit * squash).astype(BF)
        gate_act = masked * up * sig * (1.0 + gate * (1.0 - sig))
        acts_ref[...] = jnp.concatenate([gate_act, masked * act], axis=1).astype(BF)

    wide = pl.BlockSpec((tile, 2 * units), lambda i: (i, 0))
    narrow = pl.BlockSpec((tile, units), lambda i: (i, 0))
    line = pl.BlockSpec((1, units), lambda i: (0, 0))
    return pl.pallas_call(
        kernel,
        grid=(steps,),
        in_specs=[pl.BlockSpec((tile, 3 * units), lambda i: (i, 0))] * NZ + [line],
        out_specs=[wide, narrow, line],
        out_shape=[
            jax.ShapeDtypeStruct((rows, 2 * units), BF),
            jax.ShapeDtypeStruct((rows, units), BF),
            jax.ShapeDtypeStruct((1, units), F32),
        ],
        compiler_params=params(),
        cost_estimate=pl.CostEstimate(
            flops=40 * rows * units, bytes_accessed=34 * rows * units, transcendentals=2 * rows * units
        ),
    )(*parts, bound)


def input_terms(zi, pieces, own, other, ties=()):
    group, both = pieces[0].shape
    units, depth = own[0].shape
    steps = 4
    tile = 2 * depth // steps
    half = steps // 2
    rows = NZ * group

    def kernel(z_ref, *refs):
        p_refs, w_refs = refs[:NZ], refs[NZ : NZ + 4]
        out_ref, all_ref, stacked = refs[NZ + 4 + len(ties) :]
        step = pl.program_id(0)

        @pl.when(step == 0)
        def _():
            for j in range(NZ):
                start = pl.multiple_of(lax.rem(z_ref[0] + j, NZ) * group, group)
                all_ref[pl.ds(start, group), :] = p_refs[j][...]

        @pl.when(step < half)
        def _():
            stacked[:units, :] = w_refs[0][...]
            stacked[units:, :] = w_refs[1][...]

        @pl.when(step >= half)
        def _():
            stacked[:units, :] = w_refs[2][...]
            stacked[units:, :] = w_refs[3][...]

        out_ref[...] = dot(all_ref[...], stacked[...]).astype(BF)

    return pl.pallas_call(
        kernel,
        grid_spec=pltpu.PrefetchScalarGridSpec(
            num_scalar_prefetch=1,
            grid=(steps,),
            in_specs=[pl.BlockSpec((group, both), lambda i, z: (0, 0))] * NZ
            + [pl.BlockSpec((units, tile), lambda i, z: (0, jnp.minimum(i, half - 1)))] * 2
            + [pl.BlockSpec((units, tile), lambda i, z: (0, jnp.maximum(i - half, 0)))] * 2
            + [pl.BlockSpec(memory_space=pl.ANY)] * len(ties),
            out_specs=[
                pl.BlockSpec((rows, tile), lambda i, z: (0, i)),
                pl.BlockSpec((rows, both), lambda i, z: (0, 0)),
            ],
            scratch_shapes=[pltpu.VMEM((both, tile), BF)],
        ),
        out_shape=[
            jax.ShapeDtypeStruct((rows, 2 * depth), BF),
            jax.ShapeDtypeStruct((rows, both), BF),
        ],
        compiler_params=params(),
        cost_estimate=pl.CostEstimate(
            flops=4 * rows * both * depth,
            bytes_accessed=4 * rows * both + 4 * rows * depth + 4 * both * depth,
            transcendentals=0,
        ),
    )(zi, *pieces, *own, *other, *ties)


def repeated(shard, peers, ties=()):
    rows, width = shard.shape
    steps = 4

    def kernel(s_ref, *refs):
        refs[-1][...] = jnp.broadcast_to(s_ref[...][None], refs[-1].shape)

    return pl.pallas_call(
        kernel,
        grid=(steps,),
        in_specs=[pl.BlockSpec((rows, width), lambda i: (0, 0))]
        + [pl.BlockSpec(memory_space=pl.ANY)] * len(ties),
        out_specs=pl.BlockSpec((peers // steps, rows, width), lambda i: (i, 0, 0)),
        out_shape=jax.ShapeDtypeStruct((peers, rows, width), shard.dtype),
        cost_estimate=pl.CostEstimate(flops=0, bytes_accessed=2 * peers * rows * width, transcendentals=0),
    )(shard, *ties)


def summed(pieces, ties=()):
    peers, rows, width = pieces.shape
    steps = 4
    tile = width // steps

    def kernel(p_ref, *refs):
        refs[-1][...] = jnp.sum(p_ref[...].astype(F32), axis=0)

    return pl.pallas_call(
        kernel,
        grid=(steps,),
        in_specs=[pl.BlockSpec((peers, rows, tile), lambda i: (0, 0, i))]
        + [pl.BlockSpec(memory_space=pl.ANY)] * len(ties),
        out_specs=pl.BlockSpec((rows, tile), lambda i: (0, i)),
        out_shape=jax.ShapeDtypeStruct((rows, width), F32),
        cost_estimate=pl.CostEstimate(
            flops=peers * rows * width, bytes_accessed=2 * peers * rows * width, transcendentals=0
        ),
    )(pieces, *ties)


def hidden_message(first, second, tops, ties=()):
    rows, units = first.shape

    def kernel(a_ref, b_ref, s_ref, t_ref, *refs):
        out_ref = refs[-1]
        out_ref[:rows, :] = a_ref[...]
        out_ref[rows : 2 * rows, :] = b_ref[...]
        rest = jnp.maximum(s_ref[...], t_ref[...])
        addends = []
        for _ in range(3):
            addends.append(rest.astype(BF).astype(F32))
            rest = rest - addends[-1]
        line = lax.broadcasted_iota(jnp.int32, (16, units), 0)
        tail = jnp.zeros((16, units), F32)
        for i, addend in enumerate(addends):
            tail = jnp.where(line == i, addend, tail)
        out_ref[2 * rows :, :] = tail.astype(BF)

    whole = pl.BlockSpec((rows, units), lambda: (0, 0))
    one = pl.BlockSpec((1, units), lambda: (0, 0))
    return pl.pallas_call(
        kernel,
        in_specs=[whole, whole, one, one] + [pl.BlockSpec(memory_space=pl.ANY)] * len(ties),
        out_specs=pl.BlockSpec((2 * rows + 16, units), lambda: (0, 0)),
        out_shape=jax.ShapeDtypeStruct((2 * rows + 16, units), BF),
        cost_estimate=pl.CostEstimate(flops=0, bytes_accessed=8 * rows * units, transcendentals=0),
    )(first, second, *tops, *ties)


def hidden_by_z(zi, pieces, ties=()):
    units = pieces[0].shape[1]
    rows = (pieces[0].shape[0] - 16) // 2
    wide = -(-units // 128) * 128

    def kernel(z_ref, *refs):
        out_ref, top_ref = refs[-2:]
        if wide > units:
            out_ref[:, units:] = jnp.zeros((2 * NZ * rows, wide - units), BF)
        top = None
        for j in range(NZ):
            owner = lax.rem(z_ref[0] + j, NZ)
            for chunk in range(2):
                start = pl.multiple_of(chunk * NZ * rows + owner * rows, rows)
                out_ref[pl.ds(start, rows), :units] = refs[j][chunk * rows : (chunk + 1) * rows, :]
            tail = refs[j][2 * rows :, :].astype(F32)
            value = (tail[0:1] + tail[1:2]) + tail[2:3]
            top = value if top is None else jnp.maximum(top, value)
        top_ref[...] = top

    whole = pl.BlockSpec((2 * rows + 16, units), lambda i, z: (0, 0))
    return pl.pallas_call(
        kernel,
        grid_spec=pltpu.PrefetchScalarGridSpec(
            num_scalar_prefetch=1,
            grid=(1,),
            in_specs=[whole] * NZ + [pl.BlockSpec(memory_space=pl.ANY)] * len(ties),
            out_specs=[
                pl.BlockSpec((2 * NZ * rows, wide), lambda i, z: (0, 0)),
                pl.BlockSpec((1, units), lambda i, z: (0, 0)),
            ],
        ),
        out_shape=[
            jax.ShapeDtypeStruct((2 * NZ * rows, wide), BF),
            jax.ShapeDtypeStruct((1, units), F32),
        ],
        cost_estimate=pl.CostEstimate(flops=0, bytes_accessed=32 * rows * units, transcendentals=0),
    )(zi, *pieces, *ties)


def weight_gradients(terms, outs, units, depth):
    peers, few, _ = terms[0][2].shape
    rows = peers * few // 2
    wide = terms[0][0].shape[1]
    steps = 4
    tile = depth // steps
    n = len(terms)

    def kernel(*refs):
        lefts, rights, results, turned = refs[:n], refs[n : 2 * n], refs[2 * n : 2 * n + outs], refs[-1]

        @pl.when(pl.program_id(0) == 0)
        def _():
            for i in range(n):
                turned[:, i * rows : (i + 1) * rows] = lefts[i][...].T

        right = jnp.concatenate([r[...].reshape(rows, tile) for r in rights], axis=0)
        for o in range(outs):
            results[o][...] = dot(turned[o * units : (o + 1) * units, :], right).astype(BF)

    def left_spec(block):
        return pl.BlockSpec((rows, wide), lambda i: (block, 0))

    def right_spec(which, half):
        return pl.BlockSpec((peers, few // 2, tile), lambda i: (0, which, half * steps + i))

    return pl.pallas_call(
        kernel,
        grid=(steps,),
        in_specs=[left_spec(t[1]) for t in terms] + [right_spec(t[3], t[4]) for t in terms],
        out_specs=[pl.BlockSpec((units, tile), lambda i: (0, i))] * outs,
        out_shape=[jax.ShapeDtypeStruct((units, depth), BF)] * outs,
        scratch_shapes=[pltpu.VMEM((wide, n * rows), BF)],
        compiler_params=params(),
        cost_estimate=pl.CostEstimate(
            flops=2 * n * rows * wide * depth,
            bytes_accessed=2 * (n * rows * (wide + depth) + wide * depth),
            transcendentals=0,
        ),
    )(*[t[0] for t in terms], *[t[2] for t in terms])


def sum_parts(pieces):
    got = {k: shift(pieces[k], "z", k) for k in (2, 1, 3)}
    return [pieces[0]] + [got[k] for k in (1, 2, 3)]


def gather_parts(share):
    got = {j: shift(share, "z", -j) for j in (2, 1, 3)}
    return [share] + [got[j] for j in (1, 2, 3)]


def per_device(tokens, gate_weight, up_weight, down_weight, grad_mixed, amax_history):
    zi = lax.axis_index("z")
    ci = lax.axis_index("c")
    zs = zi.astype(jnp.int32).reshape((1,))
    own_rows, width = tokens.shape
    block = width // NZ
    half = block // NC
    few = NZ * NL * own_rows
    peers = NX * NY
    chunk = few // 2

    gate_t, up_t = gate_weight.T, up_weight.T
    gate_other = swap(gate_t)
    up_other = swap(up_t)
    down_other = swap(down_weight)

    def own_first(value):
        return jnp.where(ci == 0, value, jnp.concatenate([value[..., half:], value[..., :half]], axis=-1))

    both = jnp.concatenate([tokens, grad_mixed], axis=0).reshape(2 * own_rows, NZ, 1, block)
    both = jnp.broadcast_to(both.transpose(1, 2, 0, 3), (NZ, NL, 2 * own_rows, block))
    placed = own_first(exchange(both.reshape(NZ * NL, 2 * own_rows, block), ("z", "l")))
    parts = placed.reshape(2, few // 2 // own_rows, 2, own_rows, block).transpose(0, 2, 1, 3, 4)
    parts = parts.reshape(2, few, block)

    own, other = [gate_t, up_t, down_weight], [gate_other, up_other, down_other]
    bound = amax_history[None, :]

    pairs_a = exchange(repeated(parts[0], peers), ("x", "y"))
    pairs_b = exchange(repeated(parts[1], peers), ("x", "y"))
    part_a = project(zs, pairs_a, own, other)
    part_b = project(zs, pairs_b, own, other)
    acts_a, hidden_a, amax_a = activations(sum_parts(part_a), bound)
    acts_b, hidden_b, amax_b = activations(sum_parts(part_b), bound)
    terms_a, acts_all_a = input_terms(zs, gather_parts(acts_a), own[:2], other[:2], (acts_b,))
    terms_b, acts_all_b = input_terms(zs, gather_parts(acts_b), own[:2], other[:2])

    sums_a = exchange(terms_a.reshape(peers, chunk, block), ("x", "y"))
    sums_b = exchange(terms_b.reshape(peers, chunk, block), ("x", "y"))

    units = gate_t.shape[0]
    message = hidden_message(hidden_a, hidden_b, (amax_a, amax_b), (terms_b,))
    other_a, other_b = swap(pairs_a), swap(pairs_b)
    grad_gate, grad_up = weight_gradients(
        [
            (acts_all_a, 0, pairs_a, 0, 0),
            (acts_all_b, 0, pairs_b, 0, 0),
            (swap(acts_all_a), 0, other_a, 0, 1),
            (swap(acts_all_b), 0, other_b, 0, 1),
        ],
        2,
        units,
        half,
    )
    hidden_all, amax = hidden_by_z(zs, gather_parts(message), (grad_gate,))
    amax = jnp.maximum(amax, swap(amax))[0]
    hidden_other = swap(hidden_all)
    (grad_down,) = weight_gradients(
        [
            (hidden_all, 0, pairs_a, 1, 0),
            (hidden_all, 1, pairs_b, 1, 0),
            (hidden_other, 0, other_a, 1, 1),
            (hidden_other, 1, other_b, 1, 1),
        ],
        1,
        units,
        half,
    )

    mine = [summed(sums_a), summed(sums_b, (grad_gate, hidden_all))]
    back = exchange(jnp.concatenate(mine, axis=0).reshape(NZ * NL, own_rows, block), ("z", "l"))
    back = own_first(jnp.sum(back.reshape(NZ, NL, own_rows, block), axis=1).astype(BF))
    grad_tokens = back.transpose(1, 0, 2).reshape(own_rows, width)
    return (grad_tokens, grad_gate.T, grad_up.T, grad_down, amax)


def solution(mesh):
    split = Mesh(mesh.devices.reshape(NZ, NC, NX, NY, NL), AXES)
    rows, units = ("z", "c"), MP
    return jax.shard_map(
        per_device,
        mesh=split,
        in_specs=(
            P(AXES, None),
            P(rows, units),
            P(rows, units),
            P(units, rows),
            P(AXES, None),
            P(units),
        ),
        out_specs=(P(AXES, None), P(rows, units), P(rows, units), P(units, rows), P(units)),
        check_vma=False,
    )
```

```python
import jax
import jax.numpy as jnp
from jax import lax
from jax.experimental import pallas as pl
from jax.experimental.pallas import tpu as pltpu
from jax.sharding import Mesh, PartitionSpec as P

NZ, NC, NX, NY, NL = 4, 2, 4, 4, 2
AXES = ("z", "c", "x", "y", "l")
MP = ("x", "y", "l")
BF = jnp.bfloat16
F32 = jnp.float32


def shift(value, axis, k):
    n = {"z": NZ, "c": NC, "l": NL}[axis]
    return lax.ppermute(value, axis, [(i, (i + k) % n) for i in range(n)])


def swap(value):
    return shift(value, "c", 1)


def dot(left, right):
    return jnp.dot(left, right, preferred_element_type=F32)


def exchange(value, axis):
    return lax.all_to_all(value, axis, split_axis=0, concat_axis=0, tiled=True)


VMEM_BYTES = 48 * 2**20


def params():
    return pltpu.CompilerParams(vmem_limit_bytes=VMEM_BYTES)


def dot_nt(left, right):
    return lax.dot_general(left, right, (((1,), (1,)), ((), ())), preferred_element_type=F32)


def project(zi, columns, own, other, shard=None, weight=1):
    n = len(own)
    shards = [] if shard is None else [shard]
    peers, few, width = columns.shape
    rows = peers * few // 2
    units = own[0].shape[0]
    steps, group = 4, rows // NZ
    tile = width // steps

    def kernel(z_ref, a_ref, b_ref, *refs):
        own_refs, other_refs = refs[:n], refs[n : 2 * n]
        refs = refs[2 * n :]
        if shards:
            refs[1 + NZ][...] = jnp.broadcast_to(refs[0][...][None], refs[1 + NZ].shape)
        out, sends, totals = refs[len(shards)], refs[len(shards) + 1 :][: NZ - 1], refs[-n:]
        step = pl.program_id(0)
        left = jnp.concatenate([a_ref[...].reshape(rows, tile), b_ref[...].reshape(rows, tile)], axis=0)

        @pl.when(step == 0)
        def _():
            for total, w in zip(totals, own_refs):
                total[...] = dot_nt(left, w[...])

        @pl.when((step > 0) & (step < steps // 2))
        def _():
            for total, w in zip(totals, own_refs):
                total[...] += dot_nt(left, w[...])

        @pl.when(step >= steps // 2)
        def _():
            for total, w in zip(totals, other_refs):
                total[...] += dot_nt(left, w[...])

        @pl.when(step == steps - 1)
        def _():
            for k in range(NZ):
                for h in range(2):
                    start = pl.multiple_of(h * rows + lax.rem(z_ref[0] + k, NZ) * group, group)
                    parts = [total[pl.ds(start, group), :] for total in totals]
                    value = jnp.concatenate(parts, axis=1) if n > 1 else parts[0]
                    if k == 0:
                        out[h * group : (h + 1) * group, :] = value
                    else:
                        sends[k - 1][h * group : (h + 1) * group, :] = value.astype(BF)

    half = steps // 2
    whole = pl.BlockSpec((2 * group, n * units), lambda i, z: (0, 0))
    return pl.pallas_call(
        kernel,
        grid_spec=pltpu.PrefetchScalarGridSpec(
            num_scalar_prefetch=1,
            grid=(steps,),
            in_specs=[
                pl.BlockSpec((peers, few // 2, tile), lambda i, z: (0, 0, i)),
                pl.BlockSpec((peers, few // 2, tile), lambda i, z: (0, 1, i)),
            ]
            + [pl.BlockSpec((units, tile), lambda i, z: (0, jnp.minimum(i, half - 1)))] * n
            + [pl.BlockSpec((units, tile), lambda i, z: (0, jnp.maximum(i - half, 0)))] * n
            + [pl.BlockSpec((few, tile), lambda i, z: (0, i))] * len(shards),
            out_specs=[whole] * NZ
            + [pl.BlockSpec((peers, few, tile), lambda i, z: (0, 0, i))] * len(shards),
            scratch_shapes=[pltpu.VMEM((2 * rows, units), F32)] * n,
        ),
        out_shape=[jax.ShapeDtypeStruct((2 * group, n * units), F32)]
        + [jax.ShapeDtypeStruct((2 * group, n * units), BF)] * (NZ - 1)
        + [jax.ShapeDtypeStruct((peers, few, width), BF)] * len(shards),
        compiler_params=params(),
        cost_estimate=pl.CostEstimate(
            flops=weight * 4 * rows * width * units * n,
            bytes_accessed=weight * (2 * (2 * rows * width + width * units * n) + 20 * group * n * units),
            transcendentals=0,
        ),
    )(zi, columns, columns, *own, *other, *shards)


def activations(both, hidden_grad, bound, part, ties=()):
    rows, units = hidden_grad[0].shape
    rows = rows // 2
    steps = 2
    tile = rows // steps

    def kernel(*refs):
        b_refs, h_refs, bound_ref = refs[:NZ], refs[NZ : 2 * NZ], refs[2 * NZ]
        acts_ref, hidden_ref, amax_ref = refs[2 * NZ + 1 + len(ties) :]
        total = b_refs[0][...]
        for ref in b_refs[1:]:
            total = total + ref[...].astype(F32)
        grad = h_refs[0][...]
        for ref in h_refs[1:]:
            grad = grad + ref[...].astype(F32)
        gate, up = total[:, :units], total[:, units:]
        limit = bound_ref[...]
        sig = jax.nn.sigmoid(gate)
        act = gate * sig
        raw = act * up
        top = jnp.max(jnp.abs(raw), axis=0, keepdims=True)
        step = pl.program_id(0)

        @pl.when(step == 0)
        def _():
            amax_ref[...] = top

        @pl.when(step > 0)
        def _():
            amax_ref[...] = jnp.maximum(amax_ref[...], top)

        squash = jnp.tanh(raw / limit)
        masked = grad * (1.0 - squash * squash)
        hidden_ref[...] = (limit * squash).astype(BF)
        gate_act = masked * up * sig * (1.0 + gate * (1.0 - sig))
        acts_ref[...] = jnp.concatenate([gate_act, masked * act], axis=1).astype(BF)

    wide = pl.BlockSpec((tile, 2 * units), lambda i: (i, 0))
    narrow = pl.BlockSpec((tile, units), lambda i: (i, 0))
    wide_in = pl.BlockSpec((tile, 2 * units), lambda i: (part * steps + i, 0))
    narrow_in = pl.BlockSpec((tile, units), lambda i: (part * steps + i, 0))
    line = pl.BlockSpec((1, units), lambda i: (0, 0))
    return pl.pallas_call(
        kernel,
        grid=(steps,),
        in_specs=[wide_in] * NZ + [narrow_in] * NZ + [line]
        + [pl.BlockSpec(memory_space=pl.ANY)] * len(ties),
        out_specs=[wide, narrow, line],
        out_shape=[
            jax.ShapeDtypeStruct((rows, 2 * units), BF),
            jax.ShapeDtypeStruct((rows, units), BF),
            jax.ShapeDtypeStruct((1, units), F32),
        ],
        compiler_params=params(),
        cost_estimate=pl.CostEstimate(
            flops=40 * rows * units, bytes_accessed=34 * rows * units, transcendentals=2 * rows * units
        ),
    )(*both, *hidden_grad, bound, *ties)


def input_terms(zi, pieces, own, other, ties=(), weight=1):
    group, both = pieces[0].shape
    units, depth = own[0].shape
    steps = 4
    tile = 2 * depth // steps
    half = steps // 2
    rows = NZ * group

    def kernel(z_ref, *refs):
        p_refs, w_refs = refs[:NZ], refs[NZ : NZ + 4]
        out_ref, all_ref, stacked = refs[NZ + 4 + len(ties) :]
        step = pl.program_id(0)

        @pl.when(step == 0)
        def _():
            for j in range(NZ):
                start = pl.multiple_of(lax.rem(z_ref[0] + j, NZ) * group, group)
                all_ref[pl.ds(start, group), :] = p_refs[j][...]

        @pl.when(step < half)
        def _():
            stacked[:units, :] = w_refs[0][...]
            stacked[units:, :] = w_refs[1][...]

        @pl.when(step >= half)
        def _():
            stacked[:units, :] = w_refs[2][...]
            stacked[units:, :] = w_refs[3][...]

        out_ref[...] = dot(all_ref[...], stacked[...]).astype(BF)

    return pl.pallas_call(
        kernel,
        grid_spec=pltpu.PrefetchScalarGridSpec(
            num_scalar_prefetch=1,
            grid=(steps,),
            in_specs=[pl.BlockSpec((group, both), lambda i, z: (0, 0))] * NZ
            + [pl.BlockSpec((units, tile), lambda i, z: (0, jnp.minimum(i, half - 1)))] * 2
            + [pl.BlockSpec((units, tile), lambda i, z: (0, jnp.maximum(i - half, 0)))] * 2
            + [pl.BlockSpec(memory_space=pl.ANY)] * len(ties),
            out_specs=[
                pl.BlockSpec((rows, tile), lambda i, z: (0, i)),
                pl.BlockSpec((rows, both), lambda i, z: (0, 0)),
            ],
            scratch_shapes=[pltpu.VMEM((both, tile), BF)],
        ),
        out_shape=[
            jax.ShapeDtypeStruct((rows, 2 * depth), BF),
            jax.ShapeDtypeStruct((rows, both), BF),
        ],
        compiler_params=params(),
        cost_estimate=pl.CostEstimate(
            flops=weight * 4 * rows * both * depth,
            bytes_accessed=weight * (4 * rows * both + 4 * rows * depth + 4 * both * depth),
            transcendentals=0,
        ),
    )(zi, *pieces, *own, *other, *ties)


def summed(pieces, ties=()):
    peers, rows, width = pieces.shape
    steps = 2
    tile = width // steps

    def kernel(p_ref, *refs):
        refs[-1][...] = jnp.sum(p_ref[...].astype(F32), axis=0)

    return pl.pallas_call(
        kernel,
        grid=(steps,),
        in_specs=[pl.BlockSpec((peers, rows, tile), lambda i: (0, 0, i))]
        + [pl.BlockSpec(memory_space=pl.ANY)] * len(ties),
        out_specs=pl.BlockSpec((rows, tile), lambda i: (0, i)),
        out_shape=jax.ShapeDtypeStruct((rows, width), F32),
        cost_estimate=pl.CostEstimate(
            flops=peers * rows * width, bytes_accessed=2 * peers * rows * width, transcendentals=0
        ),
    )(pieces, *ties)


def hidden_message(first, second, tops, ties=()):
    rows, units = first.shape

    def kernel(a_ref, b_ref, s_ref, t_ref, *refs):
        out_ref = refs[-1]
        out_ref[:rows, :] = a_ref[...]
        out_ref[rows : 2 * rows, :] = b_ref[...]
        rest = jnp.maximum(s_ref[...], t_ref[...])
        addends = []
        for _ in range(3):
            addends.append(rest.astype(BF).astype(F32))
            rest = rest - addends[-1]
        line = lax.broadcasted_iota(jnp.int32, (16, units), 0)
        tail = jnp.zeros((16, units), F32)
        for i, addend in enumerate(addends):
            tail = jnp.where(line == i, addend, tail)
        out_ref[2 * rows :, :] = tail.astype(BF)

    whole = pl.BlockSpec((rows, units), lambda: (0, 0))
    one = pl.BlockSpec((1, units), lambda: (0, 0))
    return pl.pallas_call(
        kernel,
        in_specs=[whole, whole, one, one] + [pl.BlockSpec(memory_space=pl.ANY)] * len(ties),
        out_specs=pl.BlockSpec((2 * rows + 16, units), lambda: (0, 0)),
        out_shape=jax.ShapeDtypeStruct((2 * rows + 16, units), BF),
        cost_estimate=pl.CostEstimate(flops=0, bytes_accessed=8 * rows * units, transcendentals=0),
    )(first, second, *tops, *ties)


def hidden_by_z(zi, pieces, ties=()):
    units = pieces[0].shape[1]
    rows = (pieces[0].shape[0] - 16) // 2
    wide = -(-units // 128) * 128

    def kernel(z_ref, *refs):
        out_ref, top_ref = refs[-2:]
        if wide > units:
            out_ref[:, units:] = jnp.zeros((2 * NZ * rows, wide - units), BF)
        top = None
        for j in range(NZ):
            owner = lax.rem(z_ref[0] + j, NZ)
            for chunk in range(2):
                start = pl.multiple_of(chunk * NZ * rows + owner * rows, rows)
                out_ref[pl.ds(start, rows), :units] = refs[j][chunk * rows : (chunk + 1) * rows, :]
            tail = refs[j][2 * rows :, :].astype(F32)
            value = (tail[0:1] + tail[1:2]) + tail[2:3]
            top = value if top is None else jnp.maximum(top, value)
        top_ref[...] = top

    whole = pl.BlockSpec((2 * rows + 16, units), lambda i, z: (0, 0))
    return pl.pallas_call(
        kernel,
        grid_spec=pltpu.PrefetchScalarGridSpec(
            num_scalar_prefetch=1,
            grid=(1,),
            in_specs=[whole] * NZ + [pl.BlockSpec(memory_space=pl.ANY)] * len(ties),
            out_specs=[
                pl.BlockSpec((2 * NZ * rows, wide), lambda i, z: (0, 0)),
                pl.BlockSpec((1, units), lambda i, z: (0, 0)),
            ],
        ),
        out_shape=[
            jax.ShapeDtypeStruct((2 * NZ * rows, wide), BF),
            jax.ShapeDtypeStruct((1, units), F32),
        ],
        cost_estimate=pl.CostEstimate(flops=0, bytes_accessed=32 * rows * units, transcendentals=0),
    )(zi, *pieces, *ties)


def weight_gradients(terms, outs, units, depth):
    peers, few, _ = terms[0][2].shape
    rows = peers * few // 2
    wide = terms[0][0].shape[1]
    steps = 4
    tile = depth // steps
    n = len(terms)

    def kernel(*refs):
        lefts, rights, results, turned = refs[:n], refs[n : 2 * n], refs[2 * n : 2 * n + outs], refs[-1]

        @pl.when(pl.program_id(0) == 0)
        def _():
            for i in range(n):
                turned[:, i * rows : (i + 1) * rows] = lefts[i][...].T

        right = jnp.concatenate([r[...].reshape(rows, tile) for r in rights], axis=0)
        for o in range(outs):
            results[o][...] = dot(turned[o * units : (o + 1) * units, :], right).astype(BF)

    def left_spec(block):
        return pl.BlockSpec((rows, wide), lambda i: (block, 0))

    def right_spec(which, half):
        return pl.BlockSpec((peers, few // 2, tile), lambda i: (0, which, half * steps + i))

    return pl.pallas_call(
        kernel,
        grid=(steps,),
        in_specs=[left_spec(t[1]) for t in terms] + [right_spec(t[3], t[4]) for t in terms],
        out_specs=[pl.BlockSpec((units, tile), lambda i: (0, i))] * outs,
        out_shape=[jax.ShapeDtypeStruct((units, depth), BF)] * outs,
        scratch_shapes=[pltpu.VMEM((wide, n * rows), BF)],
        compiler_params=params(),
        cost_estimate=pl.CostEstimate(
            flops=2 * n * rows * wide * depth // 1000,
            bytes_accessed=2 * (n * rows * (wide + depth) + wide * depth) // 1000,
            transcendentals=0,
        ),
    )(*[t[0] for t in terms], *[t[2] for t in terms])


def sum_parts(pieces):
    got = {k: shift(pieces[k], "z", k) for k in (2, 1, 3)}
    return [pieces[0]] + [got[k] for k in (1, 2, 3)]


def gather_parts(share):
    got = {j: shift(share, "z", -j) for j in (2, 1, 3)}
    return [share] + [got[j] for j in (1, 2, 3)]


def per_device(tokens, gate_weight, up_weight, down_weight, grad_mixed, amax_history):
    zi = lax.axis_index("z")
    ci = lax.axis_index("c")
    zs = zi.astype(jnp.int32).reshape((1,))
    own_rows, width = tokens.shape
    block = width // NZ
    half = block // NC
    few = NZ * NL * own_rows
    peers = NX * NY

    gate_t, up_t = gate_weight.T, up_weight.T
    gate_other = swap(gate_t)
    up_other = swap(up_t)
    down_other = swap(down_weight)

    def own_first(value):
        return jnp.where(ci == 0, value, jnp.concatenate([value[..., half:], value[..., :half]], axis=-1))

    both = jnp.concatenate([tokens, grad_mixed], axis=0).reshape(2 * own_rows, NZ, 1, block)
    both = jnp.broadcast_to(both.transpose(1, 2, 0, 3), (NZ, NL, 2 * own_rows, block))
    placed = own_first(exchange(both.reshape(NZ * NL, 2 * own_rows, block), ("z", "l")))
    tokens_few = placed[:, :own_rows].reshape(few, block)
    grads_few = placed[:, own_rows:].reshape(few, block)

    own, other = [gate_t, up_t], [gate_other, up_other]
    bound = amax_history[None, :]

    tokens_all = exchange(jnp.broadcast_to(tokens_few[None], (peers, few, block)), ("x", "y"))
    *both, grads_sent = project(zs, tokens_all, own, other, grads_few)
    grads_all = exchange(grads_sent, ("x", "y"))
    hidden_grad = project(zs, grads_all, [down_weight], [down_other], None, 8)
    both, hidden_grad = sum_parts(both), sum_parts(hidden_grad)

    acts_a, hidden_a, amax_a = activations(both, hidden_grad, bound, 0)
    pieces_a = gather_parts(acts_a)
    acts_b, hidden_b, amax_b = activations(both, hidden_grad, bound, 1, pieces_a[1:])
    pieces_b = gather_parts(acts_b)
    terms_a, acts_all_a = input_terms(zs, pieces_a, own, other, (acts_b,))
    terms_b, acts_all_b = input_terms(zs, pieces_b, own, other, (), 8)
    chunk = few // 2

    sums_a = exchange(terms_a.reshape(peers, chunk, block), ("x", "y"))
    sums_b = exchange(terms_b.reshape(peers, chunk, block), ("x", "y"))

    units = gate_t.shape[0]
    message = hidden_message(hidden_a, hidden_b, (amax_a, amax_b), pieces_b[1:])
    tokens_other, grads_other = swap(tokens_all), swap(grads_all)
    grad_gate, grad_up = weight_gradients(
        [
            (acts_all_a, 0, tokens_all, 0, 0),
            (acts_all_b, 0, tokens_all, 1, 0),
            (swap(acts_all_a), 0, tokens_other, 0, 1),
            (swap(acts_all_b), 0, tokens_other, 1, 1),
        ],
        2,
        units,
        half,
    )
    hidden_all, amax = hidden_by_z(zs, gather_parts(message), (grad_gate,))
    mine = [summed(sums_a), summed(sums_b, (hidden_all,))]
    amax = jnp.maximum(amax, swap(amax))[0]
    hidden_other = swap(hidden_all)
    (grad_down,) = weight_gradients(
        [
            (hidden_all, 0, grads_all, 0, 0),
            (hidden_all, 1, grads_all, 1, 0),
            (hidden_other, 0, grads_other, 0, 1),
            (hidden_other, 1, grads_other, 1, 1),
        ],
        1,
        units,
        half,
    )

    back = exchange(jnp.concatenate(mine, axis=0).reshape(NZ * NL, own_rows, block), ("z", "l"))
    back = own_first(jnp.sum(back.reshape(NZ, NL, own_rows, block), axis=1).astype(BF))
    grad_tokens = back.transpose(1, 0, 2).reshape(own_rows, width)
    return (grad_tokens, grad_gate.T, grad_up.T, grad_down, amax)


def solution(mesh):
    split = Mesh(mesh.devices.reshape(NZ, NC, NX, NY, NL), AXES)
    rows, units = ("z", "c"), MP
    return jax.shard_map(
        per_device,
        mesh=split,
        in_specs=(
            P(AXES, None),
            P(rows, units),
            P(rows, units),
            P(units, rows),
            P(AXES, None),
            P(units),
        ),
        out_specs=(P(AXES, None), P(rows, units), P(rows, units), P(units, rows), P(units)),
        check_vma=False,
    )
```

```python
import jax
import jax.numpy as jnp
from jax import lax
from jax.experimental import pallas as pl
from jax.experimental.pallas import tpu as pltpu
from jax.sharding import Mesh, PartitionSpec as P

NZ, NC, NX, NY, NL = 4, 2, 4, 4, 2
AXES = ("z", "c", "x", "y", "l")
MP = ("x", "y", "l")
BF = jnp.bfloat16
F32 = jnp.float32


def shift(value, axis, k):
    n = {"z": NZ, "c": NC, "l": NL}[axis]
    return lax.ppermute(value, axis, [(i, (i + k) % n) for i in range(n)])


def swap(value):
    return shift(value, "c", 1)


def dot(left, right):
    return jnp.dot(left, right, preferred_element_type=F32)


def exchange(value, axis):
    return lax.all_to_all(value, axis, split_axis=0, concat_axis=0, tiled=True)


VMEM_BYTES = 48 * 2**20


def params():
    return pltpu.CompilerParams(vmem_limit_bytes=VMEM_BYTES)


def dot_nt(left, right):
    return lax.dot_general(left, right, (((1,), (1,)), ((), ())), preferred_element_type=F32)


def project(zi, columns, own, other, weight=1):
    n = len(own)
    peers, few, width = columns.shape
    rows = peers * few // 2
    units = own[0].shape[0]
    steps, group = 4, rows // NZ
    tile = width // steps

    def kernel(z_ref, a_ref, b_ref, *refs):
        own_refs, other_refs = refs[:n], refs[n : 2 * n]
        out, sends, totals = refs[2 * n], refs[2 * n + 1 : 2 * n + NZ], refs[2 * n + NZ :]
        step = pl.program_id(0)
        left = jnp.concatenate([a_ref[...].reshape(rows, tile), b_ref[...].reshape(rows, tile)], axis=0)

        @pl.when(step == 0)
        def _():
            for total, w in zip(totals, own_refs):
                total[...] = dot_nt(left, w[...])

        @pl.when((step > 0) & (step < steps // 2))
        def _():
            for total, w in zip(totals, own_refs):
                total[...] += dot_nt(left, w[...])

        @pl.when(step >= steps // 2)
        def _():
            for total, w in zip(totals, other_refs):
                total[...] += dot_nt(left, w[...])

        @pl.when(step == steps - 1)
        def _():
            for k in range(NZ):
                for h in range(2):
                    start = pl.multiple_of(h * rows + lax.rem(z_ref[0] + k, NZ) * group, group)
                    parts = [total[pl.ds(start, group), :] for total in totals]
                    value = jnp.concatenate(parts, axis=1) if n > 1 else parts[0]
                    if k == 0:
                        out[h * group : (h + 1) * group, :] = value
                    else:
                        sends[k - 1][h * group : (h + 1) * group, :] = value.astype(BF)

    half = steps // 2
    whole = pl.BlockSpec((2 * group, n * units), lambda i, z: (0, 0))
    return pl.pallas_call(
        kernel,
        grid_spec=pltpu.PrefetchScalarGridSpec(
            num_scalar_prefetch=1,
            grid=(steps,),
            in_specs=[
                pl.BlockSpec((peers, few // 2, tile), lambda i, z: (0, 0, i)),
                pl.BlockSpec((peers, few // 2, tile), lambda i, z: (0, 1, i)),
            ]
            + [pl.BlockSpec((units, tile), lambda i, z: (0, jnp.minimum(i, half - 1)))] * n
            + [pl.BlockSpec((units, tile), lambda i, z: (0, jnp.maximum(i - half, 0)))] * n,
            out_specs=[whole] * NZ,
            scratch_shapes=[pltpu.VMEM((2 * rows, units), F32)] * n,
        ),
        out_shape=[jax.ShapeDtypeStruct((2 * group, n * units), F32)]
        + [jax.ShapeDtypeStruct((2 * group, n * units), BF)] * (NZ - 1),
        compiler_params=params(),
        cost_estimate=pl.CostEstimate(
            flops=weight * 4 * rows * width * units * n,
            bytes_accessed=weight * (2 * (2 * rows * width + width * units * n) + 20 * group * n * units),
            transcendentals=0,
        ),
    )(zi, columns, columns, *own, *other)


def activations(both, hidden_grad, bound):
    n = len(both)
    rows, units = hidden_grad[0].shape
    steps = 4
    tile = rows // steps

    def kernel(*refs):
        b_refs, h_refs, bound_ref = refs[:n], refs[n : 2 * n], refs[2 * n]
        acts_ref, hidden_ref, amax_ref = refs[2 * n + 1 :]
        total = b_refs[0][...]
        for ref in b_refs[1:]:
            total = total + ref[...].astype(F32)
        grad = h_refs[0][...]
        for ref in h_refs[1:]:
            grad = grad + ref[...].astype(F32)
        gate, up = total[:, :units], total[:, units:]
        limit = bound_ref[...]
        sig = jax.nn.sigmoid(gate)
        act = gate * sig
        raw = act * up
        top = jnp.max(jnp.abs(raw), axis=0, keepdims=True)
        step = pl.program_id(0)

        @pl.when(step == 0)
        def _():
            amax_ref[...] = top

        @pl.when(step > 0)
        def _():
            amax_ref[...] = jnp.maximum(amax_ref[...], top)

        squash = jnp.tanh(raw / limit)
        masked = grad * (1.0 - squash * squash)
        hidden_ref[...] = (limit * squash).astype(BF)
        gate_act = masked * up * sig * (1.0 + gate * (1.0 - sig))
        acts_ref[...] = jnp.concatenate([gate_act, masked * act], axis=1).astype(BF)

    wide = pl.BlockSpec((tile, 2 * units), lambda i: (i, 0))
    narrow = pl.BlockSpec((tile, units), lambda i: (i, 0))
    line = pl.BlockSpec((1, units), lambda i: (0, 0))
    return pl.pallas_call(
        kernel,
        grid=(steps,),
        in_specs=[wide] * n + [narrow] * n + [line],
        out_specs=[wide, narrow, line],
        out_shape=[
            jax.ShapeDtypeStruct((rows, 2 * units), BF),
            jax.ShapeDtypeStruct((rows, units), BF),
            jax.ShapeDtypeStruct((1, units), F32),
        ],
        compiler_params=params(),
        cost_estimate=pl.CostEstimate(
            flops=40 * rows * units, bytes_accessed=34 * rows * units, transcendentals=2 * rows * units
        ),
    )(*both, *hidden_grad, bound)


def input_terms(zi, pieces, own, other, peers):
    group, both = pieces[0].shape
    group = group // 2
    units, depth = own[0].shape
    steps = 4
    tile = 2 * depth // steps
    half = steps // 2
    rows = NZ * group
    few = 2 * rows // peers

    def kernel(z_ref, *refs):
        p_refs, w_refs = refs[:NZ], refs[NZ : NZ + 4]
        out_ref, all_ref, stacked = refs[NZ + 4 :]
        step = pl.program_id(0)

        @pl.when(step == 0)
        def _():
            for j in range(NZ):
                for h in range(2):
                    start = pl.multiple_of(h * rows + lax.rem(z_ref[0] + j, NZ) * group, group)
                    all_ref[pl.ds(start, group), :] = p_refs[j][h * group : (h + 1) * group, :]

        @pl.when(step < half)
        def _():
            stacked[:units, :] = w_refs[0][...]
            stacked[units:, :] = w_refs[1][...]

        @pl.when(step >= half)
        def _():
            stacked[:units, :] = w_refs[2][...]
            stacked[units:, :] = w_refs[3][...]

        value = dot(all_ref[...], stacked[...]).astype(BF)
        for h in range(2):
            part = value[h * rows : (h + 1) * rows].reshape(peers, few // 2, tile)
            out_ref[:, h * (few // 2) : (h + 1) * (few // 2), :] = part

    return pl.pallas_call(
        kernel,
        grid_spec=pltpu.PrefetchScalarGridSpec(
            num_scalar_prefetch=1,
            grid=(steps,),
            in_specs=[pl.BlockSpec((2 * group, both), lambda i, z: (0, 0))] * NZ
            + [pl.BlockSpec((units, tile), lambda i, z: (0, jnp.minimum(i, half - 1)))] * 2
            + [pl.BlockSpec((units, tile), lambda i, z: (0, jnp.maximum(i - half, 0)))] * 2,
            out_specs=[
                pl.BlockSpec((peers, few, tile), lambda i, z: (0, 0, i)),
                pl.BlockSpec((2 * rows, both), lambda i, z: (0, 0)),
            ],
            scratch_shapes=[pltpu.VMEM((both, tile), BF)],
        ),
        out_shape=[
            jax.ShapeDtypeStruct((peers, few, 2 * depth), BF),
            jax.ShapeDtypeStruct((2 * rows, both), BF),
        ],
        compiler_params=params(),
        cost_estimate=pl.CostEstimate(
            flops=8 * rows * both * depth,
            bytes_accessed=8 * rows * both + 8 * rows * depth + 4 * both * depth,
            transcendentals=0,
        ),
    )(zi, *pieces, *own, *other)


def repeated(shard, peers, ties=()):
    rows, width = shard.shape
    steps = 4

    def kernel(s_ref, *refs):
        refs[-1][...] = jnp.broadcast_to(s_ref[...][None], refs[-1].shape)

    return pl.pallas_call(
        kernel,
        grid=(steps,),
        in_specs=[pl.BlockSpec((rows, width), lambda i: (0, 0))]
        + [pl.BlockSpec(memory_space=pl.ANY)] * len(ties),
        out_specs=pl.BlockSpec((peers // steps, rows, width), lambda i: (i, 0, 0)),
        out_shape=jax.ShapeDtypeStruct((peers, rows, width), shard.dtype),
        cost_estimate=pl.CostEstimate(flops=0, bytes_accessed=2 * peers * rows * width, transcendentals=0),
    )(shard, *ties)


def summed(pieces, ties=()):
    peers, rows, width = pieces.shape
    steps = 2
    tile = width // steps

    def kernel(p_ref, *refs):
        refs[-1][...] = jnp.sum(p_ref[...].astype(F32), axis=0)

    return pl.pallas_call(
        kernel,
        grid=(steps,),
        in_specs=[pl.BlockSpec((peers, rows, tile), lambda i: (0, 0, i))]
        + [pl.BlockSpec(memory_space=pl.ANY)] * len(ties),
        out_specs=pl.BlockSpec((rows, tile), lambda i: (0, i)),
        out_shape=jax.ShapeDtypeStruct((rows, width), F32),
        cost_estimate=pl.CostEstimate(
            flops=peers * rows * width, bytes_accessed=2 * peers * rows * width, transcendentals=0
        ),
    )(pieces, *ties)


def hidden_message(hidden, top, ties=()):
    rows, units = hidden.shape

    def kernel(a_ref, t_ref, *refs):
        out_ref = refs[-1]
        out_ref[:rows, :] = a_ref[...]
        rest = t_ref[...]
        addends = []
        for _ in range(3):
            addends.append(rest.astype(BF).astype(F32))
            rest = rest - addends[-1]
        line = lax.broadcasted_iota(jnp.int32, (16, units), 0)
        tail = jnp.zeros((16, units), F32)
        for i, addend in enumerate(addends):
            tail = jnp.where(line == i, addend, tail)
        out_ref[rows:, :] = tail.astype(BF)

    return pl.pallas_call(
        kernel,
        in_specs=[
            pl.BlockSpec((rows, units), lambda: (0, 0)),
            pl.BlockSpec((1, units), lambda: (0, 0)),
        ]
        + [pl.BlockSpec(memory_space=pl.ANY)] * len(ties),
        out_specs=pl.BlockSpec((rows + 16, units), lambda: (0, 0)),
        out_shape=jax.ShapeDtypeStruct((rows + 16, units), BF),
        cost_estimate=pl.CostEstimate(flops=0, bytes_accessed=4 * rows * units, transcendentals=0),
    )(hidden, top, *ties)


def hidden_by_z(zi, pieces, ties=()):
    units = pieces[0].shape[1]
    rows = (pieces[0].shape[0] - 16) // 2
    wide = -(-units // 128) * 128

    def kernel(z_ref, *refs):
        out_ref, top_ref = refs[-2:]
        if wide > units:
            out_ref[:, units:] = jnp.zeros((2 * NZ * rows, wide - units), BF)
        top = None
        for j in range(NZ):
            owner = lax.rem(z_ref[0] + j, NZ)
            for chunk in range(2):
                start = pl.multiple_of(chunk * NZ * rows + owner * rows, rows)
                out_ref[pl.ds(start, rows), :units] = refs[j][chunk * rows : (chunk + 1) * rows, :]
            tail = refs[j][2 * rows :, :].astype(F32)
            value = (tail[0:1] + tail[1:2]) + tail[2:3]
            top = value if top is None else jnp.maximum(top, value)
        top_ref[...] = top

    whole = pl.BlockSpec((2 * rows + 16, units), lambda i, z: (0, 0))
    return pl.pallas_call(
        kernel,
        grid_spec=pltpu.PrefetchScalarGridSpec(
            num_scalar_prefetch=1,
            grid=(1,),
            in_specs=[whole] * NZ + [pl.BlockSpec(memory_space=pl.ANY)] * len(ties),
            out_specs=[
                pl.BlockSpec((2 * NZ * rows, wide), lambda i, z: (0, 0)),
                pl.BlockSpec((1, units), lambda i, z: (0, 0)),
            ],
        ),
        out_shape=[
            jax.ShapeDtypeStruct((2 * NZ * rows, wide), BF),
            jax.ShapeDtypeStruct((1, units), F32),
        ],
        cost_estimate=pl.CostEstimate(flops=0, bytes_accessed=32 * rows * units, transcendentals=0),
    )(zi, *pieces, *ties)


def weight_gradients(terms, outs, units, depth):
    peers, few, _ = terms[0][2].shape
    rows = peers * few // 2
    wide = terms[0][0].shape[1]
    steps = 4
    tile = depth // steps
    n = len(terms)

    def kernel(*refs):
        lefts, rights, results, turned = refs[:n], refs[n : 2 * n], refs[2 * n : 2 * n + outs], refs[-1]

        @pl.when(pl.program_id(0) == 0)
        def _():
            for i in range(n):
                turned[:, i * rows : (i + 1) * rows] = lefts[i][...].T

        right = jnp.concatenate([r[...].reshape(rows, tile) for r in rights], axis=0)
        for o in range(outs):
            results[o][...] = dot(turned[o * units : (o + 1) * units, :], right).astype(BF)

    def left_spec(block):
        return pl.BlockSpec((rows, wide), lambda i: (block, 0))

    def right_spec(which, half):
        return pl.BlockSpec((peers, few // 2, tile), lambda i: (0, which, half * steps + i))

    return pl.pallas_call(
        kernel,
        grid=(steps,),
        in_specs=[left_spec(t[1]) for t in terms] + [right_spec(t[3], t[4]) for t in terms],
        out_specs=[pl.BlockSpec((units, tile), lambda i: (0, i))] * outs,
        out_shape=[jax.ShapeDtypeStruct((units, depth), BF)] * outs,
        scratch_shapes=[pltpu.VMEM((wide, n * rows), BF)],
        compiler_params=params(),
        cost_estimate=pl.CostEstimate(
            flops=2 * n * rows * wide * depth // 1000,
            bytes_accessed=2 * (n * rows * (wide + depth) + wide * depth) // 1000,
            transcendentals=0,
        ),
    )(*[t[0] for t in terms], *[t[2] for t in terms])


def sum_parts(pieces):
    got = {k: shift(pieces[k], "z", k) for k in (2, 1, 3)}
    return [pieces[0]] + [got[k] for k in (1, 2, 3)]


def gather_parts(share):
    got = {j: shift(share, "z", -j) for j in (2, 1, 3)}
    return [share] + [got[j] for j in (1, 2, 3)]


def per_device(tokens, gate_weight, up_weight, down_weight, grad_mixed, amax_history):
    zi = lax.axis_index("z")
    ci = lax.axis_index("c")
    zs = zi.astype(jnp.int32).reshape((1,))
    own_rows, width = tokens.shape
    block = width // NZ
    half = block // NC
    few = NZ * NL * own_rows
    peers = NX * NY

    gate_t, up_t = gate_weight.T, up_weight.T
    gate_other = swap(gate_t)
    up_other = swap(up_t)
    down_other = swap(down_weight)

    def own_first(value):
        return jnp.where(ci == 0, value, jnp.concatenate([value[..., half:], value[..., :half]], axis=-1))

    both = jnp.concatenate([tokens, grad_mixed], axis=0).reshape(2 * own_rows, NZ, 1, block)
    both = jnp.broadcast_to(both.transpose(1, 2, 0, 3), (NZ, NL, 2 * own_rows, block))
    placed = own_first(exchange(both.reshape(NZ * NL, 2 * own_rows, block), ("z", "l")))
    tokens_few = placed[:, :own_rows].reshape(few, block)
    grads_few = placed[:, own_rows:].reshape(few, block)

    own, other = [gate_t, up_t], [gate_other, up_other]
    bound = amax_history[None, :]

    tokens_all = exchange(jnp.broadcast_to(tokens_few[None], (peers, few, block)), ("x", "y"))
    both = project(zs, tokens_all, own, other)
    grads_all = exchange(repeated(grads_few, peers, (tokens_all,)), ("x", "y"))
    hidden_grad = project(zs, grads_all, [down_weight], [down_other], 8)
    both, hidden_grad = sum_parts(both), sum_parts(hidden_grad)

    acts, hidden, top = activations(both, hidden_grad, bound)
    pieces = gather_parts(acts)
    terms, acts_all = input_terms(zs, pieces, own, other, peers)

    sums = exchange(terms, ("x", "y"))

    units = gate_t.shape[0]
    message = hidden_message(hidden, top, pieces[1:])
    tokens_other, grads_other = swap(tokens_all), swap(grads_all)
    acts_other = swap(acts_all)
    grad_gate, grad_up = weight_gradients(
        [
            (acts_all, 0, tokens_all, 0, 0),
            (acts_all, 1, tokens_all, 1, 0),
            (acts_other, 0, tokens_other, 0, 1),
            (acts_other, 1, tokens_other, 1, 1),
        ],
        2,
        units,
        half,
    )
    hidden_all, amax = hidden_by_z(zs, gather_parts(message), (grad_gate,))
    mine = summed(sums, (grad_gate, hidden_all))
    amax = jnp.maximum(amax, swap(amax))[0]
    hidden_other = swap(hidden_all)
    (grad_down,) = weight_gradients(
        [
            (hidden_all, 0, grads_all, 0, 0),
            (hidden_all, 1, grads_all, 1, 0),
            (hidden_other, 0, grads_other, 0, 1),
            (hidden_other, 1, grads_other, 1, 1),
        ],
        1,
        units,
        half,
    )

    back = exchange(mine.reshape(NZ * NL, own_rows, block), ("z", "l"))
    back = own_first(jnp.sum(back.reshape(NZ, NL, own_rows, block), axis=1).astype(BF))
    grad_tokens = back.transpose(1, 0, 2).reshape(own_rows, width)
    return (grad_tokens, grad_gate.T, grad_up.T, grad_down, amax)


def solution(mesh):
    split = Mesh(mesh.devices.reshape(NZ, NC, NX, NY, NL), AXES)
    rows, units = ("z", "c"), MP
    return jax.shard_map(
        per_device,
        mesh=split,
        in_specs=(
            P(AXES, None),
            P(rows, units),
            P(rows, units),
            P(units, rows),
            P(AXES, None),
            P(units),
        ),
        out_specs=(P(AXES, None), P(rows, units), P(rows, units), P(units, rows), P(units)),
        check_vma=False,
    )
```

```python
import jax
import jax.numpy as jnp
from jax import lax
from jax.experimental import pallas as pl
from jax.experimental.pallas import tpu as pltpu
from jax.sharding import Mesh, PartitionSpec as P

NZ, NC, NX, NY, NL = 4, 2, 4, 4, 2
AXES = ("z", "c", "x", "y", "l")
MP = ("x", "y", "l")
BF = jnp.bfloat16
F32 = jnp.float32


def shift(value, axis, k):
    n = {"z": NZ, "c": NC, "l": NL}[axis]
    return lax.ppermute(value, axis, [(i, (i + k) % n) for i in range(n)])


def swap(value):
    return shift(value, "c", 1)


def dot(left, right):
    return jnp.dot(left, right, preferred_element_type=F32)


def exchange(value, axis):
    return lax.all_to_all(value, axis, split_axis=0, concat_axis=0, tiled=True)


VMEM_BYTES = 60 * 2**20


def params():
    return pltpu.CompilerParams(vmem_limit_bytes=VMEM_BYTES)


def dot_nt(left, right):
    return lax.dot_general(left, right, (((1,), (1,)), ((), ())), preferred_element_type=F32)


def project(zi, columns, own, other, weight=1):
    n = len(own)
    peers, few, width = columns.shape
    rows = peers * few // 2
    units = own[0].shape[0]
    steps, group = 4, rows // NZ
    tile = width // steps

    def kernel(z_ref, a_ref, b_ref, *refs):
        own_refs, other_refs = refs[:n], refs[n : 2 * n]
        out, above, below, keep_above, keep_below = refs[2 * n : 2 * n + 5]
        totals = refs[2 * n + 5 :]
        step = pl.program_id(0)
        left = jnp.concatenate([a_ref[...].reshape(rows, tile), b_ref[...].reshape(rows, tile)], axis=0)

        @pl.when(step == 0)
        def _():
            for total, w in zip(totals, own_refs):
                total[...] = dot_nt(left, w[...])

        @pl.when((step > 0) & (step < steps // 2))
        def _():
            for total, w in zip(totals, own_refs):
                total[...] += dot_nt(left, w[...])

        @pl.when(step >= steps // 2)
        def _():
            for total, w in zip(totals, other_refs):
                total[...] += dot_nt(left, w[...])

        @pl.when(step == steps - 1)
        def _():
            def rows_of(k, h):
                start = pl.multiple_of(h * rows + lax.rem(z_ref[0] + k, NZ) * group, group)
                parts = [total[pl.ds(start, group), :] for total in totals]
                return jnp.concatenate(parts, axis=1) if n > 1 else parts[0]

            first, second = pl.ds(0, group), pl.ds(group, group)
            out[first, :] = rows_of(0, 0)
            out[second, :] = rows_of(0, 1)
            above[first, :] = rows_of(2, 0).astype(BF)
            above[second, :] = rows_of(1, 1).astype(BF)
            below[first, :] = rows_of(3, 0).astype(BF)
            below[second, :] = rows_of(2, 1).astype(BF)
            keep_above[...] = rows_of(1, 0)
            keep_below[...] = rows_of(3, 1)

    half = steps // 2
    whole = pl.BlockSpec((2 * group, n * units), lambda i, z: (0, 0))
    part = pl.BlockSpec((group, n * units), lambda i, z: (0, 0))
    return pl.pallas_call(
        kernel,
        grid_spec=pltpu.PrefetchScalarGridSpec(
            num_scalar_prefetch=1,
            grid=(steps,),
            in_specs=[
                pl.BlockSpec((peers, few // 2, tile), lambda i, z: (0, 0, i)),
                pl.BlockSpec((peers, few // 2, tile), lambda i, z: (0, 1, i)),
            ]
            + [pl.BlockSpec((units, tile), lambda i, z: (0, jnp.minimum(i, half - 1)))] * n
            + [pl.BlockSpec((units, tile), lambda i, z: (0, jnp.maximum(i - half, 0)))] * n,
            out_specs=[whole] * 3 + [part] * 2,
            scratch_shapes=[pltpu.VMEM((2 * rows, units), F32)] * n,
        ),
        out_shape=[jax.ShapeDtypeStruct((2 * group, n * units), F32)]
        + [jax.ShapeDtypeStruct((2 * group, n * units), BF)] * 2
        + [jax.ShapeDtypeStruct((group, n * units), F32)] * 2,
        compiler_params=params(),
        cost_estimate=pl.CostEstimate(
            flops=weight * 4 * rows * width * units * n,
            bytes_accessed=weight * (2 * (2 * rows * width + width * units * n) + 20 * group * n * units),
            transcendentals=0,
        ),
    )(zi, columns, columns, *own, *other)


def relayed(keep_above, keep_below, from_below, from_above, ties=()):
    rows, wide = keep_above.shape

    def kernel(a_ref, b_ref, c_ref, d_ref, *refs):
        refs[-2][...] = (a_ref[...] + c_ref[...].astype(F32)).astype(BF)
        refs[-1][...] = (b_ref[...] + d_ref[...].astype(F32)).astype(BF)

    part = pl.BlockSpec((rows, wide), lambda i: (0, 0))
    return pl.pallas_call(
        kernel,
        grid=(1,),
        in_specs=[part, part, part, pl.BlockSpec((rows, wide), lambda i: (1, 0))]
        + [pl.BlockSpec(memory_space=pl.ANY)] * len(ties),
        out_specs=[part, part],
        out_shape=[jax.ShapeDtypeStruct((rows, wide), BF)] * 2,
        cost_estimate=pl.CostEstimate(flops=2 * rows * wide, bytes_accessed=16 * rows * wide, transcendentals=0),
    )(keep_above, keep_below, from_below, from_above, *ties)


def activations(both, hidden_grad, bound):
    n = len(both)
    rows, units = hidden_grad[0].shape
    steps = 4
    tile = rows // steps

    def kernel(*refs):
        b_refs, h_refs, bound_ref = refs[:n], refs[n : 2 * n], refs[2 * n]
        first_ref, second_ref, hidden_ref, amax_ref = refs[2 * n + 1 :]
        step = pl.program_id(0)

        def work(early, acts_ref):
            def added(parts):
                mine, below, above, late_below, late_above = parts
                came, late = (above, late_below) if early else (below, late_above)
                return mine[...] + came[...].astype(F32) + late[...].astype(F32)

            total, grad = added(b_refs), added(h_refs)
            gate, up = total[:, :units], total[:, units:]
            limit = bound_ref[...]
            sig = jax.nn.sigmoid(gate)
            act = gate * sig
            raw = act * up
            top = jnp.max(jnp.abs(raw), axis=0, keepdims=True)

            @pl.when(step == 0)
            def _():
                amax_ref[...] = top

            @pl.when(step > 0)
            def _():
                amax_ref[...] = jnp.maximum(amax_ref[...], top)

            squash = jnp.tanh(raw / limit)
            masked = grad * (1.0 - squash * squash)
            hidden_ref[...] = (limit * squash).astype(BF)
            gate_act = masked * up * sig * (1.0 + gate * (1.0 - sig))
            acts_ref[...] = jnp.concatenate([gate_act, masked * act], axis=1).astype(BF)

        @pl.when(step < steps // 2)
        def _():
            work(True, first_ref)

        @pl.when(step >= steps // 2)
        def _():
            work(False, second_ref)

    def half_specs(columns):
        return [
            pl.BlockSpec((tile, columns), lambda i: (jnp.minimum(i, steps // 2 - 1), 0)),
            pl.BlockSpec((tile, columns), lambda i: (jnp.maximum(i - steps // 2, 0), 0)),
        ]

    def ring_specs(columns):
        return [pl.BlockSpec((tile, columns), lambda i: (i, 0))] * 3 + half_specs(columns)

    narrow = pl.BlockSpec((tile, units), lambda i: (i, 0))
    line = pl.BlockSpec((1, units), lambda i: (0, 0))
    return pl.pallas_call(
        kernel,
        grid=(steps,),
        in_specs=ring_specs(2 * units) + ring_specs(units) + [line],
        out_specs=half_specs(2 * units) + [narrow, line],
        out_shape=[
            jax.ShapeDtypeStruct((rows // 2, 2 * units), BF),
            jax.ShapeDtypeStruct((rows // 2, 2 * units), BF),
            jax.ShapeDtypeStruct((rows, units), BF),
            jax.ShapeDtypeStruct((1, units), F32),
        ],
        compiler_params=params(),
        cost_estimate=pl.CostEstimate(
            flops=40 * rows * units, bytes_accessed=34 * rows * units, transcendentals=2 * rows * units
        ),
    )(*both, *hidden_grad, bound)


def input_terms(zi, pieces, own, other, peers):
    n = len(pieces)
    group, both = pieces[0].shape
    units, depth = own[0].shape
    steps = 4
    tile = 2 * depth // steps
    half = steps // 2
    rows = NZ * group
    few = 2 * rows // peers

    def kernel(z_ref, *refs):
        p_refs, w_refs = refs[:n], refs[n : n + 4]
        out_ref, all_ref, stacked = refs[n + 4 :]
        step = pl.program_id(0)

        @pl.when(step == 0)
        def _():
            for j in range(NZ):
                for h in range(2):
                    start = pl.multiple_of(h * rows + lax.rem(z_ref[0] + j, NZ) * group, group)
                    all_ref[pl.ds(start, group), :] = p_refs[2 * j + h][...]

        @pl.when(step < half)
        def _():
            stacked[:units, :] = w_refs[0][...]
            stacked[units:, :] = w_refs[1][...]

        @pl.when(step >= half)
        def _():
            stacked[:units, :] = w_refs[2][...]
            stacked[units:, :] = w_refs[3][...]

        value = dot(all_ref[...], stacked[...]).astype(BF)
        for h in range(2):
            part = value[h * rows : (h + 1) * rows].reshape(peers, few // 2, tile)
            out_ref[:, h * (few // 2) : (h + 1) * (few // 2), :] = part

    return pl.pallas_call(
        kernel,
        grid_spec=pltpu.PrefetchScalarGridSpec(
            num_scalar_prefetch=1,
            grid=(steps,),
            in_specs=[pl.BlockSpec((group, both), lambda i, z: (0, 0))] * n
            + [pl.BlockSpec((units, tile), lambda i, z: (0, jnp.minimum(i, half - 1)))] * 2
            + [pl.BlockSpec((units, tile), lambda i, z: (0, jnp.maximum(i - half, 0)))] * 2,
            out_specs=[
                pl.BlockSpec((peers, few, tile), lambda i, z: (0, 0, i)),
                pl.BlockSpec((2 * rows, both), lambda i, z: (0, 0)),
            ],
            scratch_shapes=[pltpu.VMEM((both, tile), BF)],
        ),
        out_shape=[
            jax.ShapeDtypeStruct((peers, few, 2 * depth), BF),
            jax.ShapeDtypeStruct((2 * rows, both), BF),
        ],
        compiler_params=params(),
        cost_estimate=pl.CostEstimate(
            flops=8 * rows * both * depth,
            bytes_accessed=8 * rows * both + 8 * rows * depth + 4 * both * depth,
            transcendentals=0,
        ),
    )(zi, *pieces, *own, *other)


def repeated(shard, peers, ties=()):
    rows, width = shard.shape
    steps = 4

    def kernel(s_ref, *refs):
        refs[-1][...] = jnp.broadcast_to(s_ref[...][None], refs[-1].shape)

    return pl.pallas_call(
        kernel,
        grid=(steps,),
        in_specs=[pl.BlockSpec((rows, width), lambda i: (0, 0))]
        + [pl.BlockSpec(memory_space=pl.ANY)] * len(ties),
        out_specs=pl.BlockSpec((peers // steps, rows, width), lambda i: (i, 0, 0)),
        out_shape=jax.ShapeDtypeStruct((peers, rows, width), shard.dtype),
        cost_estimate=pl.CostEstimate(flops=0, bytes_accessed=2 * peers * rows * width, transcendentals=0),
    )(shard, *ties)


def summed(pieces, parts, ties=()):
    peers, rows, width = pieces.shape
    steps = 2
    tile, each = width // steps, rows // parts

    def kernel(p_ref, *refs):
        value = jnp.sum(p_ref[...].astype(F32), axis=0)
        for i in range(parts):
            refs[-1][i] = value[i * each : (i + 1) * each]

    return pl.pallas_call(
        kernel,
        grid=(steps,),
        in_specs=[pl.BlockSpec((peers, rows, tile), lambda i: (0, 0, i))]
        + [pl.BlockSpec(memory_space=pl.ANY)] * len(ties),
        out_specs=pl.BlockSpec((parts, each, tile), lambda i: (0, 0, i)),
        out_shape=jax.ShapeDtypeStruct((parts, each, width), F32),
        cost_estimate=pl.CostEstimate(
            flops=peers * rows * width, bytes_accessed=2 * peers * rows * width, transcendentals=0
        ),
    )(pieces, *ties)


def over_pairs(value, ties=()):
    n, rows, width = value.shape

    def kernel(v_ref, *refs):
        for i in range(n // 2):
            refs[-1][i] = (v_ref[2 * i] + v_ref[2 * i + 1]).astype(BF)

    return pl.pallas_call(
        kernel,
        grid=(1,),
        in_specs=[pl.BlockSpec((n, rows, width), lambda i: (0, 0, 0))]
        + [pl.BlockSpec(memory_space=pl.ANY)] * len(ties),
        out_specs=pl.BlockSpec((n // 2, rows, width), lambda i: (0, 0, 0)),
        out_shape=jax.ShapeDtypeStruct((n // 2, rows, width), BF),
        cost_estimate=pl.CostEstimate(flops=0, bytes_accessed=5 * n * rows * width, transcendentals=0),
    )(value, *ties)


def hidden_message(hidden, top, ties=()):
    rows, units = hidden.shape

    def kernel(a_ref, t_ref, *refs):
        out_ref = refs[-1]
        out_ref[:rows, :] = a_ref[...]
        rest = t_ref[...]
        addends = []
        for _ in range(3):
            addends.append(rest.astype(BF).astype(F32))
            rest = rest - addends[-1]
        line = lax.broadcasted_iota(jnp.int32, (16, units), 0)
        tail = jnp.zeros((16, units), F32)
        for i, addend in enumerate(addends):
            tail = jnp.where(line == i, addend, tail)
        out_ref[rows:, :] = tail.astype(BF)

    return pl.pallas_call(
        kernel,
        in_specs=[
            pl.BlockSpec((rows, units), lambda: (0, 0)),
            pl.BlockSpec((1, units), lambda: (0, 0)),
        ]
        + [pl.BlockSpec(memory_space=pl.ANY)] * len(ties),
        out_specs=pl.BlockSpec((rows + 16, units), lambda: (0, 0)),
        out_shape=jax.ShapeDtypeStruct((rows + 16, units), BF),
        cost_estimate=pl.CostEstimate(flops=0, bytes_accessed=4 * rows * units, transcendentals=0),
    )(hidden, top, *ties)


def hidden_by_z(zi, pieces, ties=()):
    units = pieces[0].shape[1]
    rows = (pieces[0].shape[0] - 16) // 2
    wide = -(-units // 128) * 128

    def kernel(z_ref, *refs):
        out_ref, top_ref = refs[-2:]
        if wide > units:
            out_ref[:, units:] = jnp.zeros((2 * NZ * rows, wide - units), BF)
        top = None
        for j in range(NZ):
            owner = lax.rem(z_ref[0] + j, NZ)
            for chunk in range(2):
                start = pl.multiple_of(chunk * NZ * rows + owner * rows, rows)
                out_ref[pl.ds(start, rows), :units] = refs[j][chunk * rows : (chunk + 1) * rows, :]
            tail = refs[j][2 * rows :, :].astype(F32)
            value = (tail[0:1] + tail[1:2]) + tail[2:3]
            top = value if top is None else jnp.maximum(top, value)
        top_ref[...] = top

    whole = pl.BlockSpec((2 * rows + 16, units), lambda i, z: (0, 0))
    return pl.pallas_call(
        kernel,
        grid_spec=pltpu.PrefetchScalarGridSpec(
            num_scalar_prefetch=1,
            grid=(1,),
            in_specs=[whole] * NZ + [pl.BlockSpec(memory_space=pl.ANY)] * len(ties),
            out_specs=[
                pl.BlockSpec((2 * NZ * rows, wide), lambda i, z: (0, 0)),
                pl.BlockSpec((1, units), lambda i, z: (0, 0)),
            ],
        ),
        out_shape=[
            jax.ShapeDtypeStruct((2 * NZ * rows, wide), BF),
            jax.ShapeDtypeStruct((1, units), F32),
        ],
        cost_estimate=pl.CostEstimate(flops=0, bytes_accessed=32 * rows * units, transcendentals=0),
    )(zi, *pieces, *ties)


def weight_gradients(terms, outs, units, depth):
    peers, few, _ = terms[0][2].shape
    rows = peers * few // 2
    wide = terms[0][0].shape[1]
    steps = 4
    tile = depth // steps
    n = len(terms)

    def kernel(*refs):
        lefts, rights, results, turned = refs[:n], refs[n : 2 * n], refs[2 * n : 2 * n + outs], refs[-1]

        @pl.when(pl.program_id(0) == 0)
        def _():
            for i in range(n):
                turned[:, i * rows : (i + 1) * rows] = lefts[i][...].T

        right = jnp.concatenate([r[...].reshape(rows, tile) for r in rights], axis=0)
        for o in range(outs):
            results[o][...] = dot(turned[o * units : (o + 1) * units, :], right).astype(BF)

    def left_spec(block):
        return pl.BlockSpec((rows, wide), lambda i: (block, 0))

    def right_spec(which, half):
        return pl.BlockSpec((peers, few // 2, tile), lambda i: (0, which, half * steps + i))

    return pl.pallas_call(
        kernel,
        grid=(steps,),
        in_specs=[left_spec(t[1]) for t in terms] + [right_spec(t[3], t[4]) for t in terms],
        out_specs=[pl.BlockSpec((units, tile), lambda i: (0, i))] * outs,
        out_shape=[jax.ShapeDtypeStruct((units, depth), BF)] * outs,
        scratch_shapes=[pltpu.VMEM((wide, n * rows), BF)],
        compiler_params=params(),
        cost_estimate=pl.CostEstimate(
            flops=2 * n * rows * wide * depth // 1000,
            bytes_accessed=2 * (n * rows * (wide + depth) + wide * depth) // 1000,
            transcendentals=0,
        ),
    )(*[t[0] for t in terms], *[t[2] for t in terms])


def first_step(parts):
    return shift(parts[1], "z", 1), shift(parts[2], "z", -1)


def ring_parts(parts, came, ties=()):
    to_above, to_below = relayed(parts[3], parts[4], *came, ties)
    return [parts[0], *came, shift(to_above, "z", 1), shift(to_below, "z", -1)]


def gather_parts(share):
    got = {j: shift(share, "z", -j) for j in (2, 1, 3)}
    return [share] + [got[j] for j in (1, 2, 3)]


def gather_halves(first, second):
    below_first, above_second = shift(first, "z", 1), shift(second, "z", -1)
    above_first, below_second = shift(first, "z", -1), shift(second, "z", 1)
    far_first, far_second = shift(below_first, "z", 1), shift(above_second, "z", -1)
    return [first, second, above_first, above_second, far_first, far_second, below_first, below_second]


def per_device(tokens, gate_weight, up_weight, down_weight, grad_mixed, amax_history):
    zi = lax.axis_index("z")
    ci = lax.axis_index("c")
    zs = zi.astype(jnp.int32).reshape((1,))
    own_rows, width = tokens.shape
    block = width // NZ
    half = block // NC
    few = NZ * NL * own_rows
    peers = NX * NY

    gate_t, up_t = gate_weight.T, up_weight.T
    gate_other = swap(gate_t)
    up_other = swap(up_t)
    down_other = swap(down_weight)

    def own_first(value):
        return jnp.where(ci == 0, value, jnp.concatenate([value[..., half:], value[..., :half]], axis=-1))

    both = jnp.concatenate([tokens, grad_mixed], axis=0).reshape(2 * own_rows, NZ, 1, block)
    both = jnp.broadcast_to(both.transpose(1, 2, 0, 3), (NZ, NL, 2 * own_rows, block))
    placed = own_first(exchange(both.reshape(NZ * NL, 2 * own_rows, block), ("z", "l")))
    tokens_few = placed[:, :own_rows].reshape(few, block)
    grads_few = placed[:, own_rows:].reshape(few, block)

    own, other = [gate_t, up_t], [gate_other, up_other]
    bound = amax_history[None, :]

    tokens_all = exchange(jnp.broadcast_to(tokens_few[None], (peers, few, block)), ("x", "y"))
    both = project(zs, tokens_all, own, other)
    grads_all = exchange(repeated(grads_few, peers, (tokens_all,)), ("x", "y"))
    hidden_grad = project(zs, grads_all, [down_weight], [down_other], 8)
    both_came, hidden_came = first_step(both), first_step(hidden_grad)
    both = ring_parts(both, both_came, (hidden_grad[0],))
    hidden_grad = ring_parts(hidden_grad, hidden_came)

    acts_first, acts_second, hidden, top = activations(both, hidden_grad, bound)
    pieces = gather_halves(acts_first, acts_second)
    terms, acts_all = input_terms(zs, pieces, own, other, peers)

    sums = exchange(terms, ("x", "y"))

    units = gate_t.shape[0]
    message = hidden_message(hidden, top, pieces[2:])
    tokens_other, grads_other = swap(tokens_all), swap(grads_all)
    acts_other = swap(acts_all)
    grad_gate, grad_up = weight_gradients(
        [
            (acts_all, 0, tokens_all, 0, 0),
            (acts_all, 1, tokens_all, 1, 0),
            (acts_other, 0, tokens_other, 0, 1),
            (acts_other, 1, tokens_other, 1, 1),
        ],
        2,
        units,
        half,
    )
    hidden_all, amax = hidden_by_z(zs, gather_parts(message), (grad_gate,))
    mine = summed(sums, NZ * NL, (grad_gate, hidden_all))
    amax = jnp.maximum(amax, swap(amax))[0]
    hidden_other = swap(hidden_all)
    (grad_down,) = weight_gradients(
        [
            (hidden_all, 0, grads_all, 0, 0),
            (hidden_all, 1, grads_all, 1, 0),
            (hidden_other, 0, grads_other, 0, 1),
            (hidden_other, 1, grads_other, 1, 1),
        ],
        1,
        units,
        half,
    )

    back = own_first(over_pairs(exchange(mine, ("z", "l")), (grad_down,)))
    grad_tokens = back.transpose(1, 0, 2).reshape(own_rows, width)
    return (grad_tokens, grad_gate.T, grad_up.T, grad_down, amax)


def solution(mesh):
    split = Mesh(mesh.devices.reshape(NZ, NC, NX, NY, NL), AXES)
    rows, units = ("z", "c"), MP
    return jax.shard_map(
        per_device,
        mesh=split,
        in_specs=(
            P(AXES, None),
            P(rows, units),
            P(rows, units),
            P(units, rows),
            P(AXES, None),
            P(units),
        ),
        out_specs=(P(AXES, None), P(rows, units), P(rows, units), P(units, rows), P(units)),
        check_vma=False,
    )
```
